32 devices in a mesh: grp: 4 (over y, core), dev: 8 (over z, x).
Axes of the slice: x: 2, y: 2, z: 4, core: 2. Of those that a mesh axis runs over, the one named last changes fastest.
Arguments:
- pixels: bfloat16 [64, 512, 256], P('grp', 'dev'), may hold values from -16 to 16
- offsets: float32 [64, 512], P('grp', 'dev'), may hold values from -1 to 1
- first_weights: bfloat16 [3, 256, 256], replicated, may hold values from -0.21875 to 0.21875
- second_weights: bfloat16 [3, 256, 256], replicated, may hold values from -0.21875 to 0.21875
- cotangent: bfloat16 [32, 256, 256], P('grp', 'dev'), may hold values from -24 to 24
Outputs:
- grad_pixels: bfloat16 [64, 512, 256], P('grp', 'dev')
- grad_first: float32 [3, 256, 256], replicated
- grad_second: float32 [3, 256, 256], replicated
- level_out: bfloat16 [32, 256, 256], P('grp', 'dev')
The draws below stay inside these ranges and needn't reach their ends.
All inputs are finite; a program needn't handle non-finite values.
Results may differ from the reference program's by a relative error of at most 0.01.
Values may be sent and summed in bfloat16 or wider, within the bound.
A program may use at most 64 MiB of HBM per device.

```python
import math
import jax
import jax.numpy as jnp
from jax import lax

F = 256
ORDERS = 3
NX = 64
NY = 512
PX = 32
PY = 256


def draw_pixels(key, part):
    base_key = jax.random.fold_in(key, 11)
    value_key = jax.random.fold_in(base_key, 1)
    scale_key = jax.random.fold_in(base_key, 2)
    scales = jnp.exp(jax.random.uniform(scale_key, (F,), jnp.float32, math.log(0.3), math.log(3.0)))
    values = jax.random.normal(value_key, (NX, NY, F), jnp.float32) * scales
    return jnp.clip(values, -16.0, 16.0).astype(jnp.bfloat16)


def levels(key, extent, cuts, least, largest):
    def one(dim, shards_of):
        steps = jax.random.uniform(jax.random.fold_in(jax.random.fold_in(key, 6), dim), (shards_of,), jnp.float32, least / len(cuts), largest / len(cuts))
        return jnp.repeat(jnp.exp(steps), extent[dim] // shards_of).reshape((-1,) + (1,) * (len(extent) - dim - 1))

    gain = one(*cuts[0])
    for cut in cuts[1:]:
        gain = gain * one(*cut)
    return gain


def gaussian(own_key, dims, width, bound, shards=(), held_as=jnp.bfloat16):
    level = levels(own_key, dims, shards, -0.22, 0.18) if shards else 1.0
    entries = jax.random.normal(own_key, dims, jnp.float32) * width * level
    return jnp.minimum(jnp.maximum(entries, -bound), bound).astype(held_as)


def setup_inputs(seed: int = 0) -> dict:
    keys = jax.random.split(jax.random.key(seed), 6)
    pixels = draw_pixels(jax.random.fold_in(keys[5], 71), 0)
    offsets = jnp.clip(jax.random.uniform(keys[1], (NX, NY), jnp.float32, -1.0, 1.0) * levels(keys[1], (NX, NY), ((0, 4), (1, 8)), -0.4, 0.0), -1.0, 1.0)
    first_weights = gaussian(keys[2], (ORDERS, F, F), (ORDERS * F) ** -0.5, 0.21875)
    second_weights = gaussian(keys[3], (ORDERS, F, F), (ORDERS * F) ** -0.5, 0.21875)
    cotangent = gaussian(keys[4], (PX, PY, F), 4.0, 24.0, ((0, 4), (1, 8)))
    return dict(pixels=pixels, offsets=offsets, first_weights=first_weights, second_weights=second_weights, cotangent=cotangent)


NEIGHBOUR_STEPS = ((-1, 0, 1.0), (1, 0, 1.0), (0, -1, 1.0), (0, 1, 1.0), (-1, -1, 0.5), (-1, 1, 0.5), (1, -1, 0.5), (1, 1, 0.5))

def graph_parts(offsets):
    height, breadth = offsets.shape
    padded = jnp.pad(offsets, 1)
    inside = jnp.pad(jnp.ones_like(offsets), 1)
    weights = []
    degree = jnp.zeros_like(offsets)
    for row_step, col_step, coupling in NEIGHBOUR_STEPS:
        neighbour = padded[1 + row_step:1 + row_step + height, 1 + col_step:1 + col_step + breadth]
        present = inside[1 + row_step:1 + row_step + height, 1 + col_step:1 + col_step + breadth]
        weight = coupling * present * jnp.exp(-(offsets - neighbour) * (offsets - neighbour))
        weights.append(weight)
        degree = degree + weight
    return (weights, lax.rsqrt(degree))

def apply_operator(values, weights, inverse_root):
    height, breadth = inverse_root.shape
    scaled = inverse_root[:, :, None] * values.astype(jnp.float32)
    padded = jnp.pad(scaled, ((1, 1), (1, 1), (0, 0)))
    summed = jnp.zeros(scaled.shape, jnp.float32)
    for (row_step, col_step, coupling), weight in zip(NEIGHBOUR_STEPS, weights):
        summed = summed + weight[:, :, None] * padded[1 + row_step:1 + row_step + height, 1 + col_step:1 + col_step + breadth, :]
    return -inverse_root[:, :, None] * summed

def chebyshev(values, graph_data):
    first_term = apply_operator(values, *graph_data).astype(jnp.bfloat16)
    second = (2.0 * apply_operator(first_term, *graph_data) - values.astype(jnp.float32)).astype(jnp.bfloat16)
    return jnp.concatenate([values, first_term, second], axis=-1)

def project_back(inputs, weights, order_index):
    flattened = inputs.reshape(-1, inputs.shape[-1])
    result = jnp.dot(flattened, weights[order_index].T, preferred_element_type=jnp.float32)
    return result.reshape(inputs.shape[:-1] + (weights.shape[2],))

def backward_terms(cotangent, weights, graph_data):
    top_term = project_back(cotangent, weights, 2).astype(jnp.bfloat16)
    middle = (project_back(cotangent, weights, 1) + 2.0 * apply_operator(top_term, *graph_data)).astype(jnp.bfloat16)
    return project_back(cotangent, weights, 0) - top_term.astype(jnp.float32) + apply_operator(middle, *graph_data)

def reference(pixels, offsets, first_weights, second_weights, cotangent):
    features = ORDERS * F
    fine_graph = graph_parts(offsets)
    pooled_offsets = offsets.reshape(PX, 2, PY, 2).mean(axis=(1, 3))
    pooled_graph = graph_parts(pooled_offsets)
    fine_terms = chebyshev(pixels, fine_graph)
    activation = jnp.dot(fine_terms.reshape(-1, features), first_weights.reshape(features, F), preferred_element_type=jnp.float32).reshape(NX, NY, F)
    hidden = jax.nn.silu(activation)
    pooled = hidden.reshape(PX, 2, PY, 2, F).mean(axis=(1, 3)).astype(jnp.bfloat16)
    pooled_terms = chebyshev(pooled, pooled_graph)
    level_out = jnp.dot(pooled_terms.reshape(-1, features), second_weights.reshape(features, F), preferred_element_type=jnp.float32).astype(jnp.bfloat16).reshape(PX, PY, F)
    second_sum = jnp.dot(pooled_terms.reshape(-1, features).T, cotangent.reshape(-1, F), preferred_element_type=jnp.float32).reshape(ORDERS, F, F)
    pooled_grad = backward_terms(cotangent, second_weights, pooled_graph)
    spread = jnp.broadcast_to((0.25 * pooled_grad)[:, None, :, None, :], (PX, 2, PY, 2, F)).reshape(NX, NY, F)
    sigmoid = jax.nn.sigmoid(activation)
    slope_term = sigmoid * (1.0 + activation * (1.0 - sigmoid))
    act_grad = (spread * slope_term).astype(jnp.bfloat16)
    first_sum = jnp.dot(fine_terms.reshape(-1, features).T, act_grad.reshape(-1, F), preferred_element_type=jnp.float32).reshape(ORDERS, F, F)
    grad_pixels = backward_terms(act_grad, first_weights, fine_graph).astype(jnp.bfloat16)
    square_sum = jnp.sum(first_sum * first_sum) + jnp.sum(second_sum * second_sum)
    factor = jnp.minimum(1.0, 2.0 * F * lax.rsqrt(square_sum + 1e-06))
    return (grad_pixels, first_sum * factor, second_sum * factor, level_out)
```

```python
import functools

import jax
import jax.numpy as jnp
from jax import lax
from jax.experimental import pallas as pl
from jax.experimental.pallas import tpu as pltpu
from jax.sharding import PartitionSpec as P

MESH = pl.DeviceIdType.MESH
F32 = jnp.float32
BF16 = jnp.bfloat16
STEPS = (
    (-1, 0, 1.0),
    (1, 0, 1.0),
    (0, -1, 1.0),
    (0, 1, 1.0),
    (-1, -1, 0.5),
    (-1, 1, 0.5),
    (1, -1, 0.5),
    (1, 1, 0.5),
)
INDEX = {(dr, dc): k for k, (dr, dc, _) in enumerate(STEPS)}
LANES = 128
RIM = 8
FINE_UP = 6
POOL_UP = 4


def edge_coefficients(offsets, inside):
    rows = offsets.shape[0]

    def moved(x, dr, dc):
        if dr:
            x = pltpu.roll(x, (-dr) % rows, 0)
        if dc:
            x = pltpu.roll(x, (-dc) % LANES, 1)
        return x

    weights = []
    degree = jnp.zeros_like(offsets)
    for dr, dc, coupling in STEPS:
        gap = offsets - moved(offsets, dr, dc)
        weight = coupling * inside * moved(inside, dr, dc) * jnp.exp(-gap * gap)
        weights.append(weight)
        degree = degree + weight
    root = lax.rsqrt(jnp.maximum(degree, 1e-30)) * inside
    found = []
    for (dr, dc, _), weight in zip(STEPS, weights):
        value = -root * weight * moved(root, dr, dc)
        if dc:
            value = pltpu.roll(value, dc % LANES, 1)
        found.append(value)
    return found


def spread_coefficients(found, stack, turned, coefs, shift, first, last):
    rows = found[0].shape[0]
    for k, value in enumerate(found):
        stack[pl.ds(k * rows, rows), :] = value
    for b in range(stack.shape[0] // LANES):
        turned[b] = stack[pl.ds(b * LANES, LANES), :].T
    width = coefs.shape[2]
    for k in range(len(STEPS)):
        for e in range(first, last):
            block, lane = divmod(k * rows + e + shift, LANES)
            coefs[k, e] = jnp.broadcast_to(
                turned[block, pl.ds(0, width), pl.ds(lane, 1)], (width, LANES)
            )


def stencil(values, coefs, row, coef_row, half):
    lanes = pl.ds(half * LANES, LANES)
    around = [values[row + dr, :, lanes] for dr in (-1, 0, 1)]
    width = around[0].shape[0]

    def column(dc):
        total = None
        for dr in (-1, 0, 1):
            if (dr, dc) in INDEX:
                term = coefs[INDEX[dr, dc], coef_row] * around[dr + 1]
                total = term if total is None else total + term
        return total

    return pltpu.roll(column(-1), 1, 0) + column(0) + pltpu.roll(column(1), width - 1, 0)


def dot(a, b):
    return lax.dot_general(a, b, (((1,), (0,)), ((), ())), preferred_element_type=F32)


def dot_rows(a, b):
    return lax.dot_general(a, b, (((1,), (1,)), ((), ())), preferred_element_type=F32)


def dot_sum(a, b):
    return lax.dot_general(a, b, (((0,), (0,)), ((), ())), preferred_element_type=F32)


def split_dot(matrix, value):
    high = value.astype(BF16)
    low = (value - high.astype(F32)).astype(BF16)
    return dot(matrix, high) + dot(matrix, low)


def kernel(
    groups, members, chunk,
    px, off, w1, w2, cot,
    gp, gfirst, gsecond, level,
    off_own, off_in,
    px_pack, px_v, px_h, px_c,
    ct_pack, ct_v, ct_h, ct_c,
    off_ext, stack, turned, pstack, pturned, coefs, pcoefs,
    t0, t1, t2, v0, v1, slope,
    c0, cm, q0, q1, q2, z0, z1, ptop, pone, pzero, pmid, pgrad,
    ag, agm, mid,
    sums, sb, full, in_a, in_b, in_c,
    halo_send, halo_recv, sum_send, sum_recv,
):
    rows, cols, feats = px.shape
    prows, pcols = cot.shape[:2]
    width, pwidth = cols + 2 * RIM, pcols + 2 * RIM
    halves = feats // LANES
    g, d = lax.axis_index("grp"), lax.axis_index("dev")

    around = []
    for dr, dc, _ in STEPS:
        ng, nd = g + dr, d + dc
        exists = (ng >= 0) & (ng < groups) & (nd >= 0) & (nd < members)
        around.append((dr, dc, exists, (ng, nd)))
    core, quad, line = lax.rem(g, 2), (g // 2) * 2 + lax.rem(d, 2), d // 2
    lines = members // 2
    peer_a = (g + 1 - 2 * core, d)
    peers_b, peers_c = [], []
    for j in range(1, groups):
        q = lax.rem(quad + j, groups)
        peers_b.append((q, ((q // 2) * 2 + core, line * 2 + lax.rem(q, 2))))
    for j in range(1, lines):
        z = lax.rem(line + j, lines)
        peers_c.append((z, (g, z * 2 + lax.rem(d, 2))))

    barrier = pltpu.get_barrier_semaphore()
    for dr, dc, exists, peer in around:
        @pl.when(exists)
        def _():
            pl.semaphore_signal(barrier, inc=1, device_id=peer, device_id_type=MESH)
    for peer in [peer_a] + [p for _, p in peers_b] + [p for _, p in peers_c]:
        pl.semaphore_signal(barrier, inc=1, device_id=peer, device_id_type=MESH)

    off_own[...] = jnp.zeros_like(off_own)
    off_own[:, pl.ds(0, cols)] = off[...]
    for source, pack in ((px, px_pack), (cot, ct_pack)):
        edge = source.shape[1]

        def pack_pair(i, _):
            for side, start in ((0, 0), (1, edge - 16)):
                cut = 0 if side == 0 else 8
                parts = [
                    source[2 * i + s, pl.ds(start, 16), :].astype(F32)[cut : cut + 8]
                    for s in (0, 1)
                ]
                pack[side, i] = jnp.concatenate(parts, axis=0).astype(BF16)
            return 0

        lax.fori_loop(0, source.shape[0] // 2, pack_pair, 0)

    greeted = groups + lines - 1
    for dr, dc, exists, peer in around:
        greeted = greeted + jnp.where(exists, 1, 0)
    pl.semaphore_wait(barrier, greeted)

    def halo_copies(dr, dc, peer):
        k, o = INDEX[dr, dc], INDEX[-dr, -dc]
        made = []
        for a, (src, pack, up, v, h, c) in enumerate(
            ((px, px_pack, FINE_UP, px_v, px_h, px_c), (cot, ct_pack, POOL_UP, ct_v, ct_h, ct_c))
        ):
            n = src.shape[0]
            if dc == 0:
                source = src.at[pl.ds(0 if dr < 0 else n - up, up)]
                land, here = v.at[o], v.at[k]
            elif dr == 0:
                source = pack.at[0 if dc < 0 else 1]
                land, here = h.at[o - 2], h.at[k - 2]
            else:
                tiles = up // 2
                source = pack.at[
                    0 if dc < 0 else 1, pl.ds(0 if dr < 0 else n // 2 - tiles, tiles)
                ]
                land, here = c.at[o - 4], c.at[k - 4]
            made.append((a, source, land, here))
        made.append((2, off_own, off_in.at[o], off_in.at[k]))
        outgoing, incoming = [], []
        for a, source, land, here in made:
            copy = functools.partial(
                pltpu.make_async_remote_copy, src_ref=source, send_sem=halo_send.at[a, k],
                device_id=peer, device_id_type=MESH,
            )
            outgoing.append(
                functools.partial(copy, dst_ref=land, recv_sem=halo_recv.at[a, o])
            )
            incoming.append(
                (here, functools.partial(copy, dst_ref=here, recv_sem=halo_recv.at[a, k]))
            )
        return outgoing, incoming

    for dr, dc, exists, peer in around:
        @pl.when(exists)
        def _():
            for copy in reversed(halo_copies(dr, dc, peer)[0]):
                copy().start()

        @pl.when(jnp.logical_not(exists))
        def _():
            for here, _ in halo_copies(dr, dc, peer)[1]:
                here[...] = jnp.zeros(here.shape, here.dtype)

    for dr, dc, exists, peer in around:
        @pl.when(exists)
        def _():
            halo_copies(dr, dc, peer)[1][2][1]().wait_recv()

    def lay(left, own, right):
        lane = lax.broadcasted_iota(jnp.int32, own.shape, 1)
        out = jnp.where(lane < RIM, pltpu.roll(left, (RIM - cols) % LANES, 1), 0.0)
        out = jnp.where((lane >= RIM) & (lane < cols + RIM), pltpu.roll(own, RIM, 1), out)
        return jnp.where(
            (lane >= cols + RIM) & (lane < width), pltpu.roll(right, cols + RIM, 1), out
        )

    def slot(dr, dc, cut):
        return off_in[INDEX[dr, dc], cut, :]

    high, low = pl.ds(rows - 8, 8), pl.ds(0, 8)
    off_ext[pl.ds(0, 8), :] = lay(slot(-1, -1, high), slot(-1, 0, high), slot(-1, 1, high))
    off_ext[pl.ds(8, rows), :] = lay(off_in[INDEX[0, -1]], off_own[...], off_in[INDEX[0, 1]])
    off_ext[pl.ds(8 + rows, 8), :] = lay(slot(1, -1, low), slot(1, 0, low), slot(1, 1, low))

    def within(shape, row_start, col_start, row_end, col_end, used):
        r = lax.broadcasted_iota(jnp.int32, shape, 0) + row_start
        lane = lax.broadcasted_iota(jnp.int32, shape, 1)
        c = lane + col_start
        ok = (r >= 0) & (r < row_end) & (c >= 0) & (c < col_end) & (lane < used)
        return jnp.where(ok, 1.0, 0.0).astype(F32)

    offsets = off_ext[...]
    inside = within(
        offsets.shape, g * rows - 8, d * cols - RIM, groups * rows, members * cols, width
    )
    spread_coefficients(
        edge_coefficients(offsets, inside), stack, turned, coefs, 2, 1, rows + 2 * FINE_UP - 1
    )
    pshape = (prows + 2 * POOL_UP, LANES)
    a_r = lax.broadcasted_iota(jnp.int32, (pshape[0], rows + 16), 0)
    a_f = lax.broadcasted_iota(jnp.int32, (pshape[0], rows + 16), 1)
    by_row = jnp.where((a_f == 2 * a_r) | (a_f == 2 * a_r + 1), 0.5, 0.0).astype(F32)
    b_f = lax.broadcasted_iota(jnp.int32, (LANES, LANES), 0)
    b_l = lax.broadcasted_iota(jnp.int32, (LANES, LANES), 1)
    by_col = jnp.where((b_f == 2 * b_l - 8) | (b_f == 2 * b_l - 7), 0.5, 0.0).astype(F32)
    exact = functools.partial(
        jnp.dot, precision=lax.Precision.HIGHEST, preferred_element_type=F32
    )
    poffsets = exact(exact(by_row, offsets), by_col)
    pinside = within(
        pshape, g * prows - POOL_UP, d * pcols - RIM, groups * prows, members * pcols, pwidth
    )
    spread_coefficients(
        edge_coefficients(poffsets, pinside), pstack, pturned, pcoefs, 0, 1,
        prows + 2 * POOL_UP - 1,
    )

    for dr, dc, exists, peer in around:
        @pl.when(exists)
        def _():
            outgoing, incoming = halo_copies(dr, dc, peer)
            for _, copy in incoming[:2]:
                copy().wait_recv()
            for copy in outgoing:
                copy().wait_send()

    def assemble(store, start, pairs, middle, left, right):
        def pair(i, _):
            lt, rt = left(i).astype(F32), right(i).astype(F32)
            for s in (0, 1):
                row = jnp.concatenate(
                    [
                        lt[8 * s : 8 * s + 8],
                        middle(2 * i + s).astype(F32),
                        rt[8 * s : 8 * s + 8],
                    ],
                    axis=0,
                )
                store(start + 2 * i + s, row)
            return 0

        lax.fori_loop(0, pairs, pair, 0)

    def store_px(e, row):
        v0[e] = row
        t0[e] = row.astype(BF16)

    def store_cot(e, row):
        c0[e] = row.astype(BF16)

    for store, src, up, v, h, c in (
        (store_px, px, FINE_UP, px_v, px_h, px_c),
        (store_cot, cot, POOL_UP, ct_v, ct_h, ct_c),
    ):
        n = src.shape[0]
        assemble(store, 0, up // 2, lambda r: v[0, r], lambda i: c[0, i], lambda i: c[1, i])
        assemble(store, up, n // 2, lambda r: src[r], lambda i: h[0, i], lambda i: h[1, i])
        assemble(store, up + n, up // 2, lambda r: v[1, r], lambda i: c[2, i], lambda i: c[3, i])

    def fine_one(e, _):
        for half in range(halves):
            value = stencil(v0, coefs, e, e, half).astype(BF16)
            t1[e, :, pl.ds(half * LANES, LANES)] = value
            v1[e, :, pl.ds(half * LANES, LANES)] = value.astype(F32)
        return 0

    def fine_two(e, _):
        for half in range(halves):
            lanes = pl.ds(half * LANES, LANES)
            t2[e, :, lanes] = (
                2.0 * stencil(v1, coefs, e, e, half) - v0[e, :, lanes]
            ).astype(BF16)
        return 0

    lax.fori_loop(1, rows + 2 * FINE_UP - 1, fine_one, 0)
    lax.fori_loop(2, rows + 2 * FINE_UP - 2, fine_two, 0)

    def pool_matrix(shape, fine_dim):
        f = lax.broadcasted_iota(jnp.int32, shape, fine_dim)
        p = lax.broadcasted_iota(jnp.int32, shape, 1 - fine_dim)
        return jnp.where((f == 2 * p - 8) | (f == 2 * p - 7), 0.25, 0.0).astype(BF16)

    gather_pool = pool_matrix((pwidth, width), 1)
    spread_pool = pool_matrix((width, pwidth), 0)

    def activate(i, _):
        e = 2 + 4 * i
        flat = (4 * width, feats)
        a = dot(t0[pl.ds(e, 4)].reshape(flat), w1[0])
        a = a + dot(t1[pl.ds(e, 4)].reshape(flat), w1[1])
        a = a + dot(t2[pl.ds(e, 4)].reshape(flat), w1[2])
        s = jax.nn.sigmoid(a)
        slope[pl.ds(4 * i, 4)] = (s * (1.0 + a * (1.0 - s))).reshape(4, width, feats)
        hidden = a * s
        for p in (0, 1):
            both = (
                hidden[2 * p * width : (2 * p + 1) * width]
                + hidden[(2 * p + 1) * width : (2 * p + 2) * width]
            )
            value = split_dot(gather_pool, both).astype(BF16)
            q0[2 + 2 * i + p] = value
            z0[2 + 2 * i + p] = value.astype(F32)
        return 0

    lax.fori_loop(0, (prows + 4) // 2, activate, 0)

    def project_pool(i, _):
        x = c0[pl.ds(4 * i, 4)].reshape(4 * pwidth, feats)
        wide = (4, pwidth, feats)
        ptop[pl.ds(4 * i, 4)] = dot_rows(x, w2[2]).astype(BF16).astype(F32).reshape(wide)
        pone[pl.ds(4 * i, 4)] = dot_rows(x, w2[1]).reshape(wide)
        pzero[pl.ds(4 * i, 4)] = dot_rows(x, w2[0]).reshape(wide)
        return 0

    lax.fori_loop(0, (prows + 2 * POOL_UP) // 4, project_pool, 0)

    def pool_middle(e, _):
        for half in range(halves):
            lanes = pl.ds(half * LANES, LANES)
            pmid[e, :, lanes] = (
                (pone[e, :, lanes] + 2.0 * stencil(ptop, pcoefs, e, e, half))
                .astype(BF16)
                .astype(F32)
            )
        return 0

    def pool_grad(e, _):
        for half in range(halves):
            lanes = pl.ds(half * LANES, LANES)
            pgrad[e, :, lanes] = (
                pzero[e, :, lanes] - ptop[e, :, lanes] + stencil(pmid, pcoefs, e, e, half)
            )
        return 0

    lax.fori_loop(2, prows + 2 * POOL_UP - 2, pool_middle, 0)
    lax.fori_loop(3, prows + 2 * POOL_UP - 3, pool_grad, 0)

    col = lax.broadcasted_iota(jnp.int32, (width, feats), 0)
    own_cols = (col >= RIM) & (col < cols + RIM)

    def act_grad(i, _):
        wide = split_dot(spread_pool, pgrad[i + 3])
        for s in (0, 1):
            value = wide * slope[2 * i + 2 + s]
            ag[2 * i + s] = value.astype(BF16)
            agm[2 * i + s] = jnp.where(own_cols, value, 0.0).astype(BF16)
        return 0

    lax.fori_loop(0, prows + 2, act_grad, 0)

    def pool_one(e, _):
        for half in range(halves):
            lanes = pl.ds(half * LANES, LANES)
            value = stencil(z0, pcoefs, e, e, half).astype(BF16)
            q1[e, :, lanes] = value
            z1[e, :, lanes] = value.astype(F32)
        return 0

    def pool_two(e, _):
        for half in range(halves):
            lanes = pl.ds(half * LANES, LANES)
            q2[e, :, lanes] = (
                2.0 * stencil(z1, pcoefs, e, e, half) - z0[e, :, lanes]
            ).astype(BF16)
        return 0

    lax.fori_loop(POOL_UP - 1, prows + POOL_UP + 1, pool_one, 0)
    lax.fori_loop(POOL_UP, prows + POOL_UP, pool_two, 0)

    pcol = lax.broadcasted_iota(jnp.int32, (pwidth, feats), 0)
    own_pcols = (pcol >= RIM) & (pcol < pcols + RIM)

    def mask_cot(r, _):
        cm[r] = jnp.where(own_pcols, c0[POOL_UP + r].astype(F32), 0.0).astype(BF16)
        return 0

    lax.fori_loop(0, prows, mask_cot, 0)

    if sums.shape[0] > 6 * feats:
        sums[pl.ds(6 * feats, sums.shape[0] - 6 * feats), :] = jnp.zeros(
            (sums.shape[0] - 6 * feats, feats), F32
        )
    back = agm[pl.ds(2, rows)].reshape(rows * width, feats)
    for k, term in enumerate((t0, t1, t2)):
        x = term[pl.ds(FINE_UP, rows)].reshape(rows * width, feats)
        sums[pl.ds(k * feats, feats), :] = dot_sum(x, back)
    pback = cm[...].reshape(prows * pwidth, feats)
    for k, term in enumerate((q0, q1, q2)):
        x = term[pl.ds(POOL_UP, prows)].reshape(prows * pwidth, feats)
        sums[pl.ds((3 + k) * feats, feats), :] = dot_sum(x, pback)

    total = sums.shape[0]
    half_rows = total // 2
    block_rows = half_rows // groups

    def at(start, size):
        return pl.ds(pl.multiple_of(start, 16), size)

    def send(number, source, target, peer):
        return pltpu.make_async_remote_copy(
            src_ref=source, dst_ref=target, send_sem=sum_send.at[number],
            recv_sem=sum_recv.at[number], device_id=peer, device_id_type=MESH,
        )

    base_a = core * half_rows
    base_b = base_a + quad * block_rows
    base_c = base_b + line * chunk
    sb[...] = sums[...].astype(BF16)
    number = 0
    stage = [send(0, sb.at[at((1 - core) * half_rows, half_rows)], in_a, peer_a)]
    stage[0].start()

    top, one, zero = v0, v1, slope

    def project_fine(i, _):
        x = ag[pl.ds(4 * i, 4)].reshape(4 * width, feats)
        wide = (4, width, feats)
        top[pl.ds(4 * i, 4)] = dot_rows(x, w1[2]).astype(BF16).astype(F32).reshape(wide)
        one[pl.ds(4 * i, 4)] = dot_rows(x, w1[1]).reshape(wide)
        zero[pl.ds(4 * i, 4)] = dot_rows(x, w1[0]).reshape(wide)
        return 0

    lax.fori_loop(0, (rows + 4) // 4, project_fine, 0)

    stage[0].wait()
    own = sums[at(base_a, half_rows), :] + in_a[...].astype(F32)
    sums[at(base_a, half_rows), :] = own
    sb[at(base_a, half_rows), :] = own.astype(BF16)
    stage = []
    for j, (q, peer) in enumerate(peers_b):
        number += 1
        stage.append(
            send(number, sb.at[at(base_a + q * block_rows, block_rows)], in_b.at[j], peer)
        )
        stage[-1].start()

    def fine_middle(a, _):
        for half in range(halves):
            lanes = pl.ds(half * LANES, LANES)
            mid[a, :, lanes] = (
                (one[a, :, lanes] + 2.0 * stencil(top, coefs, a, a + 4, half))
                .astype(BF16)
                .astype(F32)
            )
        return 0

    lax.fori_loop(1, rows + 3, fine_middle, 0)

    for copy in stage:
        copy.wait()
    own = sums[at(base_b, block_rows), :]
    for j in range(len(peers_b)):
        own = own + in_b[j].astype(F32)
    sums[at(base_b, block_rows), :] = own
    sb[at(base_b, block_rows), :] = own.astype(BF16)
    stage = []
    for j, (z, peer) in enumerate(peers_c):
        number += 1
        stage.append(send(number, sb.at[at(base_b + z * chunk, chunk)], in_c.at[j], peer))
        stage[-1].start()

    def fine_grad(a, _):
        for half in range(halves):
            lanes = pl.ds(half * LANES, LANES)
            value = (
                zero[a, :, lanes] - top[a, :, lanes] + stencil(mid, coefs, a, a + 4, half)
            )
            gp[a - 2, :, lanes] = value[RIM : RIM + cols].astype(BF16)
        return 0

    lax.fori_loop(2, rows + 2, fine_grad, 0)

    for copy in stage:
        copy.wait()
    own = sums[at(base_c, chunk), :]
    for j in range(len(peers_c)):
        own = own + in_c[j].astype(F32)
    full[at(base_c, chunk), :] = own.astype(BF16)

    stages = (
        (base_c, chunk, [p for _, p in peers_c]),
        (base_b, block_rows, [p for _, p in peers_b]),
        (base_a, half_rows, [peer_a]),
    )
    for start, size, peers in stages:
        stage = []
        for peer in peers:
            number += 1
            region = full.at[at(start, size)]
            stage.append(send(number, region, region, peer))
            stage[-1].start()
        for copy in stage:
            copy.wait()

    squares = jnp.zeros((8, feats), F32)
    for k in range(6):
        x = full[pl.ds(k * feats, feats), :].astype(F32)
        squares = squares + jnp.sum((x * x).reshape(feats // 8, 8, feats), axis=0)
    square_sum = jnp.sum(jnp.sum(squares, axis=0, keepdims=True), axis=1, keepdims=True)
    factor = jnp.minimum(1.0, 2.0 * feats * lax.rsqrt(square_sum + 1e-06))
    for k in range(3):
        rows_k = pl.ds(k * feats, feats)
        gfirst[rows_k, :] = full[rows_k, :].astype(F32) * factor
        gsecond[rows_k, :] = full[pl.ds((3 + k) * feats, feats), :].astype(F32) * factor

    for r in range(prows):
        out = dot(q0[POOL_UP + r], w2[0]) + dot(q1[POOL_UP + r], w2[1])
        out = out + dot(q2[POOL_UP + r], w2[2])
        level[r] = out[RIM : RIM + pcols].astype(BF16)


def shards(groups, members, pixels, offsets, first_weights, second_weights, cotangent):
    rows, cols, feats = pixels.shape
    prows, pcols = cotangent.shape[:2]
    width, pwidth = cols + 2 * RIM, pcols + 2 * RIM
    high, phigh, bhigh = rows + 2 * FINE_UP, prows + 2 * POOL_UP, rows + 4
    count = groups * members
    chunk = -(-6 * feats // (count * 16)) * 16
    total = chunk * count
    half = total // 2
    lines = members // 2
    orders = len(STEPS)

    def blocks(n):
        return -(-orders * n // LANES)

    nf, np_ = blocks(rows + 16), blocks(phigh)
    vm = pltpu.VMEM

    def halo(n, up, c):
        return [
            vm((2, n // 2, 16, feats), BF16),
            vm((2, up, c, feats), BF16),
            vm((2, n // 2, 16, feats), BF16),
            vm((4, up // 2, 16, feats), BF16),
        ]

    scratch = [vm((rows, LANES), F32), vm((orders, rows, LANES), F32)]
    scratch += halo(rows, FINE_UP, cols) + halo(prows, POOL_UP, pcols)
    scratch += [
        vm((rows + 16, LANES), F32),
        vm((nf * LANES, LANES), F32), vm((nf, LANES, LANES), F32),
        vm((np_ * LANES, LANES), F32), vm((np_, LANES, LANES), F32),
        vm((orders, high, width, LANES), F32), vm((orders, phigh, pwidth, LANES), F32),
    ]
    scratch += [vm((high, width, feats), t) for t in (BF16, BF16, BF16, F32, F32)]
    scratch += [vm((rows + 8, width, feats), F32)]
    scratch += [vm((phigh, pwidth, feats), BF16), vm((prows, pwidth, feats), BF16)]
    scratch += [vm((phigh, pwidth, feats), t) for t in (BF16,) * 3 + (F32,) * 7]
    scratch += [vm((bhigh, width, feats), t) for t in (BF16, BF16, F32)]
    scratch += [
        vm((total, feats), F32), vm((total, feats), BF16), vm((total, feats), BF16),
        vm((half, feats), BF16),
        vm((groups - 1, half // groups, feats), BF16),
        vm((lines - 1, chunk, feats), BF16),
    ]
    copies = 2 * (groups + lines - 1)
    scratch += [pltpu.SemaphoreType.DMA((3, orders))] * 2
    scratch += [pltpu.SemaphoreType.DMA((copies,))] * 2
    grad_pixels, first, second, level = pl.pallas_call(
        functools.partial(kernel, groups, members, chunk),
        out_shape=(
            jax.ShapeDtypeStruct(pixels.shape, BF16),
            jax.ShapeDtypeStruct((3 * feats, feats), F32),
            jax.ShapeDtypeStruct((3 * feats, feats), F32),
            jax.ShapeDtypeStruct(cotangent.shape, BF16),
        ),
        in_specs=[pl.BlockSpec(memory_space=pltpu.VMEM)] * 5,
        out_specs=[pl.BlockSpec(memory_space=pltpu.VMEM)] * 4,
        scratch_shapes=scratch,
        compiler_params=pltpu.CompilerParams(
            collective_id=0, has_side_effects=True, vmem_limit_bytes=60 * 1024 * 1024
        ),
    )(pixels, offsets, first_weights, second_weights, cotangent)
    shape = first_weights.shape
    return grad_pixels, first.reshape(shape), second.reshape(shape), level


def solution(mesh):
    groups, members = mesh.shape["grp"], mesh.shape["dev"]
    return jax.shard_map(
        functools.partial(shards, groups, members),
        mesh=mesh,
        in_specs=(P("grp", "dev", None), P("grp", "dev"), P(), P(), P("grp", "dev", None)),
        out_specs=(P("grp", "dev", None), P(), P(), P("grp", "dev", None)),
        check_vma=False,
    )
```

```python
import functools

import jax
import jax.numpy as jnp
from jax import lax
from jax.experimental import pallas as pl
from jax.experimental.pallas import tpu as pltpu
from jax.sharding import PartitionSpec as P

MESH = pl.DeviceIdType.MESH
F32 = jnp.float32
BF16 = jnp.bfloat16
STEPS = (
    (-1, 0, 1.0),
    (1, 0, 1.0),
    (0, -1, 1.0),
    (0, 1, 1.0),
    (-1, -1, 0.5),
    (-1, 1, 0.5),
    (1, -1, 0.5),
    (1, 1, 0.5),
)
INDEX = {(dr, dc): k for k, (dr, dc, _) in enumerate(STEPS)}
LANES = 128
RIM = 8
FINE_UP = 6
POOL_UP = 4


def edge_coefficients(offsets, inside):
    rows = offsets.shape[0]

    def moved(x, dr, dc):
        if dr:
            x = pltpu.roll(x, (-dr) % rows, 0)
        if dc:
            x = pltpu.roll(x, (-dc) % LANES, 1)
        return x

    weights = []
    degree = jnp.zeros_like(offsets)
    for dr, dc, coupling in STEPS:
        gap = offsets - moved(offsets, dr, dc)
        weight = coupling * inside * moved(inside, dr, dc) * jnp.exp(-gap * gap)
        weights.append(weight)
        degree = degree + weight
    root = lax.rsqrt(jnp.maximum(degree, 1e-30)) * inside
    found = []
    for (dr, dc, _), weight in zip(STEPS, weights):
        value = -root * weight * moved(root, dr, dc)
        if dc:
            value = pltpu.roll(value, dc % LANES, 1)
        found.append(value)
    return found


def spread_coefficients(found, stack, turned, coefs, shift, first, last):
    rows = found[0].shape[0]
    for k, value in enumerate(found):
        stack[pl.ds(k * rows, rows), :] = value
    for b in range(stack.shape[0] // LANES):
        turned[b] = stack[pl.ds(b * LANES, LANES), :].T
    width = coefs.shape[2]
    for k in range(len(STEPS)):
        for e in range(first, last):
            block, lane = divmod(k * rows + e + shift, LANES)
            coefs[k, e] = jnp.broadcast_to(
                turned[block, pl.ds(0, width), pl.ds(lane, 1)], (width, LANES)
            )


def stencil(values, coefs, row, coef_row, half):
    lanes = pl.ds(half * LANES, LANES)
    around = [values[row + dr, :, lanes] for dr in (-1, 0, 1)]
    width = around[0].shape[0]

    def column(dc):
        total = None
        for dr in (-1, 0, 1):
            if (dr, dc) in INDEX:
                term = coefs[INDEX[dr, dc], coef_row] * around[dr + 1]
                total = term if total is None else total + term
        return total

    return pltpu.roll(column(-1), 1, 0) + column(0) + pltpu.roll(column(1), width - 1, 0)


def dot(a, b):
    return lax.dot_general(a, b, (((1,), (0,)), ((), ())), preferred_element_type=F32)


def dot_rows(a, b):
    return lax.dot_general(a, b, (((1,), (1,)), ((), ())), preferred_element_type=F32)


def dot_sum(a, b):
    return lax.dot_general(a, b, (((0,), (0,)), ((), ())), preferred_element_type=F32)


def split_dot(matrix, value):
    high = value.astype(BF16)
    low = (value - high.astype(F32)).astype(BF16)
    return dot(matrix, high) + dot(matrix, low)


def kernel(
    groups, members, chunk,
    px, off, w1, w2, cot,
    gp, full, level,
    off_own, off_in,
    px_pack, px_v, px_h, px_c,
    ct_pack, ct_v, ct_h, ct_c,
    off_ext, stack, turned, pstack, pturned, coefs, pcoefs,
    t0, t1, t2, v0, v1, slope,
    c0, cm, q0, q1, q2, z0, z1, ptop, pone, pzero, pmid, pgrad,
    ag, agm, mid,
    sums, sb, in_a, in_b, in_c,
    halo_send, halo_recv, sum_send, sum_recv,
):
    rows, cols, feats = px.shape
    prows, pcols = cot.shape[:2]
    width, pwidth = cols + 2 * RIM, pcols + 2 * RIM
    halves = feats // LANES
    g, d = lax.axis_index("grp"), lax.axis_index("dev")

    around = []
    for dr, dc, _ in STEPS:
        ng, nd = g + dr, d + dc
        exists = (ng >= 0) & (ng < groups) & (nd >= 0) & (nd < members)
        around.append((dr, dc, exists, (ng, nd)))
    core, quad, line = lax.rem(g, 2), (g // 2) * 2 + lax.rem(d, 2), d // 2
    lines = members // 2
    peer_a = (g + 1 - 2 * core, d)
    peers_b, peers_c = [], []
    for j in range(1, groups):
        q = lax.rem(quad + j, groups)
        peers_b.append((q, ((q // 2) * 2 + core, line * 2 + lax.rem(q, 2))))
    for j in range(1, lines):
        z = lax.rem(line + j, lines)
        peers_c.append((z, (g, z * 2 + lax.rem(d, 2))))

    barrier = pltpu.get_barrier_semaphore()
    for dr, dc, exists, peer in around:
        @pl.when(exists)
        def _():
            pl.semaphore_signal(barrier, inc=1, device_id=peer, device_id_type=MESH)
    for peer in [peer_a] + [p for _, p in peers_b] + [p for _, p in peers_c]:
        pl.semaphore_signal(barrier, inc=1, device_id=peer, device_id_type=MESH)

    off_own[...] = jnp.zeros_like(off_own)
    off_own[:, pl.ds(0, cols)] = off[...]
    for source, pack in ((px, px_pack), (cot, ct_pack)):
        edge = source.shape[1]

        def pack_pair(i, _):
            for side, start in ((0, 0), (1, edge - 16)):
                cut = 0 if side == 0 else 8
                parts = [
                    source[2 * i + s, pl.ds(start, 16), :].astype(F32)[cut : cut + 8]
                    for s in (0, 1)
                ]
                pack[side, i] = jnp.concatenate(parts, axis=0).astype(BF16)
            return 0

        lax.fori_loop(0, source.shape[0] // 2, pack_pair, 0)

    greeted = groups + lines - 1
    for dr, dc, exists, peer in around:
        greeted = greeted + jnp.where(exists, 1, 0)
    pl.semaphore_wait(barrier, greeted)

    def halo_copies(dr, dc, peer):
        k, o = INDEX[dr, dc], INDEX[-dr, -dc]
        made = []
        for a, (src, pack, up, v, h, c) in enumerate(
            ((px, px_pack, FINE_UP, px_v, px_h, px_c), (cot, ct_pack, POOL_UP, ct_v, ct_h, ct_c))
        ):
            n = src.shape[0]
            if dc == 0:
                source = src.at[pl.ds(0 if dr < 0 else n - up, up)]
                land, here = v.at[o], v.at[k]
            elif dr == 0:
                source = pack.at[0 if dc < 0 else 1]
                land, here = h.at[o - 2], h.at[k - 2]
            else:
                tiles = up // 2
                source = pack.at[
                    0 if dc < 0 else 1, pl.ds(0 if dr < 0 else n // 2 - tiles, tiles)
                ]
                land, here = c.at[o - 4], c.at[k - 4]
            made.append((a, source, land, here))
        made.append((2, off_own, off_in.at[o], off_in.at[k]))
        outgoing, incoming = [], []
        for a, source, land, here in made:
            copy = functools.partial(
                pltpu.make_async_remote_copy, src_ref=source, send_sem=halo_send.at[a, k],
                device_id=peer, device_id_type=MESH,
            )
            outgoing.append(
                functools.partial(copy, dst_ref=land, recv_sem=halo_recv.at[a, o])
            )
            incoming.append(
                (here, functools.partial(copy, dst_ref=here, recv_sem=halo_recv.at[a, k]))
            )
        return outgoing, incoming

    for a in (2, 1, 0):
        for dr, dc, exists, peer in around:
            @pl.when(exists)
            def _():
                halo_copies(dr, dc, peer)[0][a]().start()

    for dr, dc, exists, peer in around:
        @pl.when(jnp.logical_not(exists))
        def _():
            for here, _ in halo_copies(dr, dc, peer)[1]:
                here[...] = jnp.zeros(here.shape, here.dtype)

    def receive(a):
        for dr, dc, exists, peer in around:
            @pl.when(exists)
            def _():
                halo_copies(dr, dc, peer)[1][a][1]().wait_recv()

    receive(2)

    def lay(left, own, right):
        lane = lax.broadcasted_iota(jnp.int32, own.shape, 1)
        out = jnp.where(lane < RIM, pltpu.roll(left, (RIM - cols) % LANES, 1), 0.0)
        out = jnp.where((lane >= RIM) & (lane < cols + RIM), pltpu.roll(own, RIM, 1), out)
        return jnp.where(
            (lane >= cols + RIM) & (lane < width), pltpu.roll(right, cols + RIM, 1), out
        )

    def slot(dr, dc, cut):
        return off_in[INDEX[dr, dc], cut, :]

    high, low = pl.ds(rows - 8, 8), pl.ds(0, 8)
    off_ext[pl.ds(0, 8), :] = lay(slot(-1, -1, high), slot(-1, 0, high), slot(-1, 1, high))
    off_ext[pl.ds(8, rows), :] = lay(off_in[INDEX[0, -1]], off_own[...], off_in[INDEX[0, 1]])
    off_ext[pl.ds(8 + rows, 8), :] = lay(slot(1, -1, low), slot(1, 0, low), slot(1, 1, low))

    def within(shape, row_start, col_start, row_end, col_end, used):
        r = lax.broadcasted_iota(jnp.int32, shape, 0) + row_start
        lane = lax.broadcasted_iota(jnp.int32, shape, 1)
        c = lane + col_start
        ok = (r >= 0) & (r < row_end) & (c >= 0) & (c < col_end) & (lane < used)
        return jnp.where(ok, 1.0, 0.0).astype(F32)

    offsets = off_ext[...]
    inside = within(
        offsets.shape, g * rows - 8, d * cols - RIM, groups * rows, members * cols, width
    )
    pshape = (prows + 2 * POOL_UP, LANES)
    a_r = lax.broadcasted_iota(jnp.int32, (pshape[0], rows + 16), 0)
    a_f = lax.broadcasted_iota(jnp.int32, (pshape[0], rows + 16), 1)
    by_row = jnp.where((a_f == 2 * a_r) | (a_f == 2 * a_r + 1), 0.5, 0.0).astype(F32)
    b_f = lax.broadcasted_iota(jnp.int32, (LANES, LANES), 0)
    b_l = lax.broadcasted_iota(jnp.int32, (LANES, LANES), 1)
    by_col = jnp.where((b_f == 2 * b_l - 8) | (b_f == 2 * b_l - 7), 0.5, 0.0).astype(F32)
    exact = functools.partial(
        jnp.dot, precision=lax.Precision.HIGHEST, preferred_element_type=F32
    )
    poffsets = exact(exact(by_row, offsets), by_col)
    pinside = within(
        pshape, g * prows - POOL_UP, d * pcols - RIM, groups * prows, members * pcols, pwidth
    )
    spread_coefficients(
        edge_coefficients(poffsets, pinside), pstack, pturned, pcoefs, 0, 1,
        prows + 2 * POOL_UP - 1,
    )

    def assemble(store, start, pairs, middle, left, right):
        def pair(i, _):
            lt, rt = left(i).astype(F32), right(i).astype(F32)
            for s in (0, 1):
                row = jnp.concatenate(
                    [
                        lt[8 * s : 8 * s + 8],
                        middle(2 * i + s).astype(F32),
                        rt[8 * s : 8 * s + 8],
                    ],
                    axis=0,
                )
                store(start + 2 * i + s, row)
            return 0

        lax.fori_loop(0, pairs, pair, 0)

    def store_px(e, row):
        v0[e] = row
        t0[e] = row.astype(BF16)

    def store_cot(e, row):
        c0[e] = row.astype(BF16)

    def assemble_all(store, src, up, v, h, c):
        n = src.shape[0]
        assemble(store, 0, up // 2, lambda r: v[0, r], lambda i: c[0, i], lambda i: c[1, i])
        assemble(store, up, n // 2, lambda r: src[r], lambda i: h[0, i], lambda i: h[1, i])
        assemble(store, up + n, up // 2, lambda r: v[1, r], lambda i: c[2, i], lambda i: c[3, i])

    receive(1)
    assemble_all(store_cot, cot, POOL_UP, ct_v, ct_h, ct_c)

    def project_pool(i, _):
        x = c0[pl.ds(4 * i, 4)].reshape(4 * pwidth, feats)
        wide = (4, pwidth, feats)
        ptop[pl.ds(4 * i, 4)] = dot_rows(x, w2[2]).astype(BF16).astype(F32).reshape(wide)
        pone[pl.ds(4 * i, 4)] = dot_rows(x, w2[1]).reshape(wide)
        pzero[pl.ds(4 * i, 4)] = dot_rows(x, w2[0]).reshape(wide)
        return 0

    lax.fori_loop(0, (prows + 2 * POOL_UP) // 4, project_pool, 0)

    def pool_middle(e, _):
        for half in range(halves):
            lanes = pl.ds(half * LANES, LANES)
            pmid[e, :, lanes] = (
                (pone[e, :, lanes] + 2.0 * stencil(ptop, pcoefs, e, e, half))
                .astype(BF16)
                .astype(F32)
            )
        return 0

    def pool_grad(e, _):
        for half in range(halves):
            lanes = pl.ds(half * LANES, LANES)
            pgrad[e, :, lanes] = (
                pzero[e, :, lanes] - ptop[e, :, lanes] + stencil(pmid, pcoefs, e, e, half)
            )
        return 0

    lax.fori_loop(2, prows + 2 * POOL_UP - 2, pool_middle, 0)
    lax.fori_loop(3, prows + 2 * POOL_UP - 3, pool_grad, 0)

    spread_coefficients(
        edge_coefficients(offsets, inside), stack, turned, coefs, 2, 1, rows + 2 * FINE_UP - 1
    )
    receive(0)
    assemble_all(store_px, px, FINE_UP, px_v, px_h, px_c)

    def fine_one(e, _):
        for half in range(halves):
            value = stencil(v0, coefs, e, e, half).astype(BF16)
            t1[e, :, pl.ds(half * LANES, LANES)] = value
            v1[e, :, pl.ds(half * LANES, LANES)] = value.astype(F32)
        return 0

    def fine_two(e, _):
        for half in range(halves):
            lanes = pl.ds(half * LANES, LANES)
            t2[e, :, lanes] = (
                2.0 * stencil(v1, coefs, e, e, half) - v0[e, :, lanes]
            ).astype(BF16)
        return 0

    lax.fori_loop(1, rows + 2 * FINE_UP - 1, fine_one, 0)
    lax.fori_loop(2, rows + 2 * FINE_UP - 2, fine_two, 0)

    def pool_matrix(shape, fine_dim):
        f = lax.broadcasted_iota(jnp.int32, shape, fine_dim)
        p = lax.broadcasted_iota(jnp.int32, shape, 1 - fine_dim)
        return jnp.where((f == 2 * p - 8) | (f == 2 * p - 7), 0.25, 0.0).astype(BF16)

    gather_pool = pool_matrix((pwidth, width), 1)
    spread_pool = pool_matrix((width, pwidth), 0)

    def activate(i, _):
        e = 2 + 4 * i
        flat = (4 * width, feats)
        a = dot(t0[pl.ds(e, 4)].reshape(flat), w1[0])
        a = a + dot(t1[pl.ds(e, 4)].reshape(flat), w1[1])
        a = a + dot(t2[pl.ds(e, 4)].reshape(flat), w1[2])
        s = jax.nn.sigmoid(a)
        slope[pl.ds(4 * i, 4)] = (s * (1.0 + a * (1.0 - s))).reshape(4, width, feats)
        hidden = a * s
        for p in (0, 1):
            both = (
                hidden[2 * p * width : (2 * p + 1) * width]
                + hidden[(2 * p + 1) * width : (2 * p + 2) * width]
            )
            value = split_dot(gather_pool, both).astype(BF16)
            q0[2 + 2 * i + p] = value
            z0[2 + 2 * i + p] = value.astype(F32)
        return 0

    lax.fori_loop(0, (prows + 4) // 2, activate, 0)

    col = lax.broadcasted_iota(jnp.int32, (width, feats), 0)
    own_cols = (col >= RIM) & (col < cols + RIM)

    def act_grad(i, _):
        wide = split_dot(spread_pool, pgrad[i + 3])
        for s in (0, 1):
            value = wide * slope[2 * i + 2 + s]
            ag[2 * i + s] = value.astype(BF16)
            agm[2 * i + s] = jnp.where(own_cols, value, 0.0).astype(BF16)
        return 0

    lax.fori_loop(0, prows + 2, act_grad, 0)

    def pool_one(e, _):
        for half in range(halves):
            lanes = pl.ds(half * LANES, LANES)
            value = stencil(z0, pcoefs, e, e, half).astype(BF16)
            q1[e, :, lanes] = value
            z1[e, :, lanes] = value.astype(F32)
        return 0

    def pool_two(e, _):
        for half in range(halves):
            lanes = pl.ds(half * LANES, LANES)
            q2[e, :, lanes] = (
                2.0 * stencil(z1, pcoefs, e, e, half) - z0[e, :, lanes]
            ).astype(BF16)
        return 0

    batch = sums.shape[0] // 2
    half_rows = batch // 2
    block_rows = half_rows // groups
    parts = 3 * feats * halves

    def at(start, size):
        return pl.ds(pl.multiple_of(start, 16), size)

    numbers = iter(range(sum_send.shape[0]))

    def send(source, target, peer):
        number = next(numbers)
        copy = pltpu.make_async_remote_copy(
            src_ref=source, dst_ref=target, send_sem=sum_send.at[number],
            recv_sem=sum_recv.at[number], device_id=peer, device_id_type=MESH,
        )
        copy.start()
        return copy

    def starts(t):
        base_a = t * batch + core * half_rows
        base_b = base_a + quad * block_rows
        return base_a, base_b, base_b + line * chunk

    def patch_sums(t, terms, first, count, back):
        if batch > parts:
            rest = batch - parts
            sb[pl.ds(t * batch + parts, rest), :] = jnp.zeros((rest, LANES), BF16)
            sums[pl.ds(t * batch + parts, rest), :] = jnp.zeros((rest, LANES), F32)
        for k, term in enumerate(terms):
            x = term[pl.ds(first, count)].reshape(back.shape[0], feats)
            value = dot_sum(x, back)
            for half in range(halves):
                place = pl.ds(t * batch + (half * 3 + k) * feats, feats)
                part = value[:, half * LANES : (half + 1) * LANES]
                sums[place, :] = part
                sb[place, :] = part.astype(BF16)

    def start_a(t):
        other = at(t * batch + (1 - core) * half_rows, half_rows)
        return [send(sb.at[other], in_a.at[t], peer_a)]

    def add(copies, start, size, landed):
        for copy in copies:
            copy.wait()
        own = sums[at(start, size), :]
        for j in range(len(copies)):
            own = own + landed(j).astype(F32)
        return own

    def a_to_b(t, copies):
        base_a, base_b, _ = starts(t)
        own = add(copies, base_a, half_rows, lambda j: in_a[t])
        sums[at(base_a, half_rows), :] = own
        sb[at(base_a, half_rows), :] = own.astype(BF16)
        return [
            send(sb.at[at(base_a + q * block_rows, block_rows)], in_b.at[t, j], peer)
            for j, (q, peer) in enumerate(peers_b)
        ]

    def b_to_c(t, copies):
        _, base_b, _ = starts(t)
        own = add(copies, base_b, block_rows, lambda j: in_b[t, j])
        sums[at(base_b, block_rows), :] = own
        sb[at(base_b, block_rows), :] = own.astype(BF16)
        return [
            send(sb.at[at(base_b + z * chunk, chunk)], in_c.at[t, j], peer)
            for j, (z, peer) in enumerate(peers_c)
        ]

    def c_to_c(t, copies):
        base_c = starts(t)[2]
        full[at(base_c, chunk), :] = add(
            copies, base_c, chunk, lambda j: in_c[t, j]
        ).astype(BF16)
        region = full.at[at(base_c, chunk)]
        return [send(region, region, peer) for _, peer in peers_c]

    def c_to_b(t, copies):
        for copy in copies:
            copy.wait()
        region = full.at[at(starts(t)[1], block_rows)]
        return [send(region, region, peer) for _, peer in peers_b], send(region, region, peer_a)

    def b_to_a(t, copies):
        copies, first = copies
        onward = [first]
        for j, copy in enumerate(copies):
            copy.wait()
            came = lax.rem(quad + groups - 1 - j, groups)
            region = full.at[at(starts(t)[0] + came * block_rows, block_rows)]
            onward.append(send(region, region, peer_a))
        return onward

    back = agm[pl.ds(2, rows)].reshape(rows * width, feats)
    patch_sums(0, (t0, t1, t2), FINE_UP, rows, back)
    fine = start_a(0)

    lax.fori_loop(POOL_UP - 1, prows + POOL_UP + 1, pool_one, 0)
    fine = a_to_b(0, fine)
    lax.fori_loop(POOL_UP, prows + POOL_UP, pool_two, 0)
    pcol = lax.broadcasted_iota(jnp.int32, (pwidth, feats), 0)
    own_pcols = (pcol >= RIM) & (pcol < pcols + RIM)

    def mask_cot(r, _):
        cm[r] = jnp.where(own_pcols, c0[POOL_UP + r].astype(F32), 0.0).astype(BF16)
        return 0

    lax.fori_loop(0, prows, mask_cot, 0)

    patch_sums(1, (q0, q1, q2), POOL_UP, prows, cm[...].reshape(prows * pwidth, feats))
    pool = start_a(1)

    top, one, zero = v0, v1, slope

    def project_fine(i, _):
        x = ag[pl.ds(4 * i, 4)].reshape(4 * width, feats)
        wide = (4, width, feats)
        top[pl.ds(4 * i, 4)] = dot_rows(x, w1[2]).astype(BF16).astype(F32).reshape(wide)
        one[pl.ds(4 * i, 4)] = dot_rows(x, w1[1]).reshape(wide)
        zero[pl.ds(4 * i, 4)] = dot_rows(x, w1[0]).reshape(wide)
        return 0

    def fine_middle(a, _):
        for half in range(halves):
            lanes = pl.ds(half * LANES, LANES)
            mid[a, :, lanes] = (
                (one[a, :, lanes] + 2.0 * stencil(top, coefs, a, a + 4, half))
                .astype(BF16)
                .astype(F32)
            )
        return 0

    def fine_grad(a, _):
        for half in range(halves):
            lanes = pl.ds(half * LANES, LANES)
            value = (
                zero[a, :, lanes] - top[a, :, lanes] + stencil(mid, coefs, a, a + 4, half)
            )
            gp[a - 2, :, lanes] = value[RIM : RIM + cols].astype(BF16)
        return 0

    lax.fori_loop(0, (rows + 4) // 4, project_fine, 0)
    pool = a_to_b(1, pool)
    fine = b_to_c(0, fine)
    lax.fori_loop(1, rows + 3, fine_middle, 0)
    fine = c_to_c(0, fine)
    pool = b_to_c(1, pool)
    lax.fori_loop(2, rows // 2 + 2, fine_grad, 0)
    fine = c_to_b(0, fine)
    pool = c_to_c(1, pool)
    lax.fori_loop(rows // 2 + 2, rows + 2, fine_grad, 0)
    pool = c_to_b(1, pool)

    flat = (prows * pwidth, feats)
    out = dot(q0[pl.ds(POOL_UP, prows)].reshape(flat), w2[0])
    out = out + dot(q1[pl.ds(POOL_UP, prows)].reshape(flat), w2[1])
    out = out + dot(q2[pl.ds(POOL_UP, prows)].reshape(flat), w2[2])
    for r in range(prows):
        start = r * pwidth + RIM
        level[r] = out[start : start + pcols].astype(BF16)

    fine = b_to_a(0, fine)
    pool = b_to_a(1, pool)
    for copy in fine + pool:
        copy.wait()
    for dr, dc, exists, peer in around:
        @pl.when(exists)
        def _():
            for copy in halo_copies(dr, dc, peer)[0]:
                copy().wait_send()


def finish(full, gp, level, gp_out, gfirst, gsecond, level_out):
    feats = gfirst.shape[1]
    halves = feats // LANES
    batch = full.shape[0] // 2
    count = gfirst.shape[0]
    gp_out[...] = gp[...]
    level_out[...] = level[...]
    squares = jnp.zeros((8, LANES), F32)
    for t in range(2):
        x = full[pl.ds(t * batch, count * halves), :].astype(F32)
        squares = squares + jnp.sum((x * x).reshape(count * halves // 8, 8, LANES), axis=0)
    square_sum = jnp.sum(jnp.sum(squares, axis=0, keepdims=True), axis=1, keepdims=True)
    factor = jnp.minimum(1.0, 2.0 * feats * lax.rsqrt(square_sum + 1e-06))
    for t, out in enumerate((gfirst, gsecond)):
        for half in range(halves):
            x = full[pl.ds(t * batch + half * count, count), :].astype(F32)
            out[:, pl.ds(half * LANES, LANES)] = x * factor


def shards(groups, members, pixels, offsets, first_weights, second_weights, cotangent):
    rows, cols, feats = pixels.shape
    prows, pcols = cotangent.shape[:2]
    width, pwidth = cols + 2 * RIM, pcols + 2 * RIM
    high, phigh, bhigh = rows + 2 * FINE_UP, prows + 2 * POOL_UP, rows + 4
    count = groups * members
    chunk = -(-3 * feats * (feats // LANES) // (count * 16)) * 16
    total = chunk * count
    half = total // 2
    lines = members // 2
    orders = len(STEPS)

    def blocks(n):
        return -(-orders * n // LANES)

    nf, np_ = blocks(rows + 16), blocks(phigh)
    vm = pltpu.VMEM

    def halo(n, up, c):
        return [
            vm((2, n // 2, 16, feats), BF16),
            vm((2, up, c, feats), BF16),
            vm((2, n // 2, 16, feats), BF16),
            vm((4, up // 2, 16, feats), BF16),
        ]

    scratch = [vm((rows, LANES), F32), vm((orders, rows, LANES), F32)]
    scratch += halo(rows, FINE_UP, cols) + halo(prows, POOL_UP, pcols)
    scratch += [
        vm((rows + 16, LANES), F32),
        vm((nf * LANES, LANES), F32), vm((nf, LANES, LANES), F32),
        vm((np_ * LANES, LANES), F32), vm((np_, LANES, LANES), F32),
        vm((orders, high, width, LANES), F32), vm((orders, phigh, pwidth, LANES), F32),
    ]
    scratch += [vm((high, width, feats), t) for t in (BF16, BF16, BF16, F32, F32)]
    scratch += [vm((rows + 8, width, feats), F32)]
    scratch += [vm((phigh, pwidth, feats), BF16), vm((prows, pwidth, feats), BF16)]
    scratch += [vm((phigh, pwidth, feats), t) for t in (BF16,) * 3 + (F32,) * 7]
    scratch += [vm((bhigh, width, feats), t) for t in (BF16, BF16, F32)]
    scratch += [
        vm((2 * total, LANES), F32), vm((2 * total, LANES), BF16),
        vm((2, half, LANES), BF16),
        vm((2, groups - 1, half // groups, LANES), BF16),
        vm((2, lines - 1, chunk, LANES), BF16),
    ]
    scratch += [pltpu.SemaphoreType.DMA((3, orders))] * 2
    copies = 2 * (3 * groups + 2 * lines - 3)
    scratch += [pltpu.SemaphoreType.DMA((copies,))] * 2
    inner_pixels, full, inner_level = pl.pallas_call(
        functools.partial(kernel, groups, members, chunk),
        out_shape=(
            jax.ShapeDtypeStruct(pixels.shape, BF16),
            jax.ShapeDtypeStruct((2 * total, LANES), BF16),
            jax.ShapeDtypeStruct(cotangent.shape, BF16),
        ),
        in_specs=[pl.BlockSpec(memory_space=pltpu.VMEM)] * 5,
        out_specs=[pl.BlockSpec(memory_space=pltpu.VMEM)] * 3,
        scratch_shapes=scratch,
        compiler_params=pltpu.CompilerParams(
            collective_id=0, has_side_effects=True, vmem_limit_bytes=60 * 1024 * 1024
        ),
    )(pixels, offsets, first_weights, second_weights, cotangent)
    grad_pixels, first, second, level = pl.pallas_call(
        finish,
        out_shape=(
            jax.ShapeDtypeStruct(pixels.shape, BF16),
            jax.ShapeDtypeStruct((3 * feats, feats), F32),
            jax.ShapeDtypeStruct((3 * feats, feats), F32),
            jax.ShapeDtypeStruct(cotangent.shape, BF16),
        ),
        in_specs=[pl.BlockSpec(memory_space=pltpu.VMEM)] * 3,
        out_specs=[pl.BlockSpec(memory_space=pltpu.VMEM)] * 4,
        compiler_params=pltpu.CompilerParams(vmem_limit_bytes=40 * 1024 * 1024),
    )(full, inner_pixels, inner_level)
    shape = first_weights.shape
    return grad_pixels, first.reshape(shape), second.reshape(shape), level


def solution(mesh):
    groups, members = mesh.shape["grp"], mesh.shape["dev"]
    return jax.shard_map(
        functools.partial(shards, groups, members),
        mesh=mesh,
        in_specs=(P("grp", "dev", None), P("grp", "dev"), P(), P(), P("grp", "dev", None)),
        out_specs=(P("grp", "dev", None), P(), P(), P("grp", "dev", None)),
        check_vma=False,
    )
```

```python
import functools

import jax
import jax.numpy as jnp
from jax import lax
from jax.experimental import pallas as pl
from jax.experimental.pallas import tpu as pltpu
from jax.sharding import PartitionSpec as P

MESH = pl.DeviceIdType.MESH
F32 = jnp.float32
BF16 = jnp.bfloat16
STEPS = (
    (-1, 0, 1.0),
    (1, 0, 1.0),
    (0, -1, 1.0),
    (0, 1, 1.0),
    (-1, -1, 0.5),
    (-1, 1, 0.5),
    (1, -1, 0.5),
    (1, 1, 0.5),
)
INDEX = {(dr, dc): k for k, (dr, dc, _) in enumerate(STEPS)}
LANES = 128
RIM = 8
FINE_UP = 6
POOL_UP = 4


def edge_coefficients(offsets, inside):
    rows = offsets.shape[0]

    def moved(x, dr, dc):
        if dr:
            x = pltpu.roll(x, (-dr) % rows, 0)
        if dc:
            x = pltpu.roll(x, (-dc) % LANES, 1)
        return x

    weights = []
    degree = jnp.zeros_like(offsets)
    for dr, dc, coupling in STEPS:
        gap = offsets - moved(offsets, dr, dc)
        weight = coupling * inside * moved(inside, dr, dc) * jnp.exp(-gap * gap)
        weights.append(weight)
        degree = degree + weight
    root = lax.rsqrt(jnp.maximum(degree, 1e-30)) * inside
    found = []
    for (dr, dc, _), weight in zip(STEPS, weights):
        value = -root * weight * moved(root, dr, dc)
        if dc:
            value = pltpu.roll(value, dc % LANES, 1)
        found.append(value)
    return found


def spread_coefficients(found, stack, turned, coefs, shift, first, last):
    rows = found[0].shape[0]
    for k, value in enumerate(found):
        stack[pl.ds(k * rows, rows), :] = value
    for b in range(stack.shape[0] // LANES):
        turned[b] = stack[pl.ds(b * LANES, LANES), :].T
    width = coefs.shape[2]
    for k in range(len(STEPS)):
        for e in range(first, last):
            block, lane = divmod(k * rows + e + shift, LANES)
            coefs[k, e] = jnp.broadcast_to(
                turned[block, pl.ds(0, width), pl.ds(lane, 1)], (width, LANES)
            )


def stencil(values, coefs, row, coef_row, half):
    lanes = pl.ds(half * LANES, LANES)
    around = [values[row + dr, :, lanes] for dr in (-1, 0, 1)]
    width = around[0].shape[0]

    def column(dc):
        total = None
        for dr in (-1, 0, 1):
            if (dr, dc) in INDEX:
                term = coefs[INDEX[dr, dc], coef_row] * around[dr + 1]
                total = term if total is None else total + term
        return total

    return pltpu.roll(column(-1), 1, 0) + column(0) + pltpu.roll(column(1), width - 1, 0)


def by_rows(first, last, work):
    def two(i, _):
        e = first + 2 * i
        for store in work(e) + work(e + 1):
            store()
        return 0

    lax.fori_loop(0, (last - first) // 2, two, 0)
    if (last - first) % 2:
        for store in work(last - 1):
            store()


def storing(ref, index, value):
    def store():
        ref[index] = value.astype(ref.dtype)

    return store


def dot(a, b):
    return lax.dot_general(a, b, (((1,), (0,)), ((), ())), preferred_element_type=F32)


def split_dot(matrix, values):
    value = jnp.concatenate(values, axis=1)
    high = value.astype(BF16)
    low = (value - high.astype(F32)).astype(BF16)
    return dot(matrix, jnp.concatenate([high, low], axis=0))


def kernel(
    groups, members, chunk,
    px, off, w1, w2, cot,
    gp, full, level,
    off_own, off_in,
    px_pack, px_v, px_h, px_c,
    ct_pack, ct_v, ct_h, ct_c,
    off_ext, stack, turned, pstack, pturned, coefs, pcoefs,
    t0, t1, t2, v0, v1, slope,
    c0, cm, q0, q1, q2, z0, z1, ptop, pone, pzero, pmid, pgrad,
    ag, agm, mid, w1t, w2t, turned_back,
    sums, sb, in_a, in_b, in_c,
    halo_send, halo_recv, sum_send, sum_recv,
):
    rows, cols, feats = px.shape
    prows, pcols = cot.shape[:2]
    width, pwidth = cols + 2 * RIM, pcols + 2 * RIM
    halves = feats // LANES
    g, d = lax.axis_index("grp"), lax.axis_index("dev")

    around = []
    for dr, dc, _ in STEPS:
        ng, nd = g + dr, d + dc
        exists = (ng >= 0) & (ng < groups) & (nd >= 0) & (nd < members)
        around.append((dr, dc, exists, (ng, nd)))
    core, quad, line = lax.rem(g, 2), (g // 2) * 2 + lax.rem(d, 2), d // 2
    lines = members // 2
    peer_a = (g + 1 - 2 * core, d)
    peers_b, peers_c = [], []
    for j in range(1, groups):
        q = lax.rem(quad + j, groups)
        peers_b.append((q, ((q // 2) * 2 + core, line * 2 + lax.rem(q, 2))))
    for j in range(1, lines):
        z = lax.rem(line + j, lines)
        peers_c.append((z, (g, z * 2 + lax.rem(d, 2))))

    barrier = pltpu.get_barrier_semaphore()
    for dr, dc, exists, peer in around:
        @pl.when(exists)
        def _():
            pl.semaphore_signal(barrier, inc=1, device_id=peer, device_id_type=MESH)
    for peer in [peer_a] + [p for _, p in peers_b] + [p for _, p in peers_c]:
        pl.semaphore_signal(barrier, inc=1, device_id=peer, device_id_type=MESH)

    off_own[...] = jnp.zeros_like(off_own)
    off_own[:, pl.ds(0, cols)] = off[...]
    for source, pack in ((px, px_pack), (cot, ct_pack)):
        edge = source.shape[1]

        def pack_pair(i, _):
            for side, start in ((0, 0), (1, edge - 16)):
                cut = 0 if side == 0 else 8
                parts = [
                    source[2 * i + s, pl.ds(start, 16), :].astype(F32)[cut : cut + 8]
                    for s in (0, 1)
                ]
                pack[side, i] = jnp.concatenate(parts, axis=0).astype(BF16)
            return 0

        lax.fori_loop(0, source.shape[0] // 2, pack_pair, 0)

    greeted = groups + lines - 1
    for dr, dc, exists, peer in around:
        greeted = greeted + jnp.where(exists, 1, 0)
    pl.semaphore_wait(barrier, greeted)

    def halo_copies(dr, dc, peer):
        k, o = INDEX[dr, dc], INDEX[-dr, -dc]
        made = []
        for a, (src, pack, up, v, h, c) in enumerate(
            ((px, px_pack, FINE_UP, px_v, px_h, px_c), (cot, ct_pack, POOL_UP, ct_v, ct_h, ct_c))
        ):
            n = src.shape[0]
            if dc == 0:
                source = src.at[pl.ds(0 if dr < 0 else n - up, up)]
                land, here = v.at[o], v.at[k]
            elif dr == 0:
                source = pack.at[0 if dc < 0 else 1]
                land, here = h.at[o - 2], h.at[k - 2]
            else:
                tiles = up // 2
                source = pack.at[
                    0 if dc < 0 else 1, pl.ds(0 if dr < 0 else n // 2 - tiles, tiles)
                ]
                land, here = c.at[o - 4], c.at[k - 4]
            made.append((a, source, land, here))
        made.append((2, off_own, off_in.at[o], off_in.at[k]))
        outgoing, incoming = [], []
        for a, source, land, here in made:
            copy = functools.partial(
                pltpu.make_async_remote_copy, src_ref=source, send_sem=halo_send.at[a, k],
                device_id=peer, device_id_type=MESH,
            )
            outgoing.append(
                functools.partial(copy, dst_ref=land, recv_sem=halo_recv.at[a, o])
            )
            incoming.append(
                (here, functools.partial(copy, dst_ref=here, recv_sem=halo_recv.at[a, k]))
            )
        return outgoing, incoming

    for a in (2, 1, 0):
        for dr, dc, exists, peer in around:
            @pl.when(exists)
            def _():
                halo_copies(dr, dc, peer)[0][a]().start()

    for dr, dc, exists, peer in around:
        @pl.when(jnp.logical_not(exists))
        def _():
            for here, _ in halo_copies(dr, dc, peer)[1]:
                here[...] = jnp.zeros(here.shape, here.dtype)

    def receive(a):
        for dr, dc, exists, peer in around:
            @pl.when(exists)
            def _():
                halo_copies(dr, dc, peer)[1][a][1]().wait_recv()

    for source, target in ((w2, w2t), (w1, w1t)):
        for k in range(source.shape[0]):
            target[:, pl.ds(k * feats, feats)] = source[k].T
    receive(2)

    def lay(left, own, right):
        lane = lax.broadcasted_iota(jnp.int32, own.shape, 1)
        out = jnp.where(lane < RIM, pltpu.roll(left, (RIM - cols) % LANES, 1), 0.0)
        out = jnp.where((lane >= RIM) & (lane < cols + RIM), pltpu.roll(own, RIM, 1), out)
        return jnp.where(
            (lane >= cols + RIM) & (lane < width), pltpu.roll(right, cols + RIM, 1), out
        )

    def slot(dr, dc, cut):
        return off_in[INDEX[dr, dc], cut, :]

    high, low = pl.ds(rows - 8, 8), pl.ds(0, 8)
    off_ext[pl.ds(0, 8), :] = lay(slot(-1, -1, high), slot(-1, 0, high), slot(-1, 1, high))
    off_ext[pl.ds(8, rows), :] = lay(off_in[INDEX[0, -1]], off_own[...], off_in[INDEX[0, 1]])
    off_ext[pl.ds(8 + rows, 8), :] = lay(slot(1, -1, low), slot(1, 0, low), slot(1, 1, low))

    def within(shape, row_start, col_start, row_end, col_end, used):
        r = lax.broadcasted_iota(jnp.int32, shape, 0) + row_start
        lane = lax.broadcasted_iota(jnp.int32, shape, 1)
        c = lane + col_start
        ok = (r >= 0) & (r < row_end) & (c >= 0) & (c < col_end) & (lane < used)
        return jnp.where(ok, 1.0, 0.0).astype(F32)

    offsets = off_ext[...]
    inside = within(
        offsets.shape, g * rows - 8, d * cols - RIM, groups * rows, members * cols, width
    )
    pshape = (prows + 2 * POOL_UP, LANES)
    a_r = lax.broadcasted_iota(jnp.int32, (pshape[0], rows + 16), 0)
    a_f = lax.broadcasted_iota(jnp.int32, (pshape[0], rows + 16), 1)
    by_row = jnp.where((a_f == 2 * a_r) | (a_f == 2 * a_r + 1), 0.5, 0.0).astype(F32)
    b_f = lax.broadcasted_iota(jnp.int32, (LANES, LANES), 0)
    b_l = lax.broadcasted_iota(jnp.int32, (LANES, LANES), 1)
    by_col = jnp.where((b_f == 2 * b_l - 8) | (b_f == 2 * b_l - 7), 0.5, 0.0).astype(F32)
    exact = functools.partial(
        jnp.dot, precision=lax.Precision.HIGHEST, preferred_element_type=F32
    )
    poffsets = exact(exact(by_row, offsets), by_col)
    pinside = within(
        pshape, g * prows - POOL_UP, d * pcols - RIM, groups * prows, members * pcols, pwidth
    )
    spread_coefficients(
        edge_coefficients(poffsets, pinside), pstack, pturned, pcoefs, 0, 1,
        prows + 2 * POOL_UP - 1,
    )

    def assemble(store, start, pairs, middle, left, right):
        def pair(i, _):
            lt, rt = left(i).astype(F32), right(i).astype(F32)
            for s in (0, 1):
                row = jnp.concatenate(
                    [
                        lt[8 * s : 8 * s + 8],
                        middle(2 * i + s).astype(F32),
                        rt[8 * s : 8 * s + 8],
                    ],
                    axis=0,
                )
                store(start + 2 * i + s, row)
            return 0

        lax.fori_loop(0, pairs, pair, 0)

    def store_px(e, row):
        v0[e] = row
        t0[e] = row.astype(BF16)

    def store_cot(e, row):
        c0[e] = row.astype(BF16)

    def assemble_all(store, src, up, v, h, c):
        n = src.shape[0]
        assemble(store, 0, up // 2, lambda r: v[0, r], lambda i: c[0, i], lambda i: c[1, i])
        assemble(store, up, n // 2, lambda r: src[r], lambda i: h[0, i], lambda i: h[1, i])
        assemble(store, up + n, up // 2, lambda r: v[1, r], lambda i: c[2, i], lambda i: c[3, i])

    receive(1)
    assemble_all(store_cot, cot, POOL_UP, ct_v, ct_h, ct_c)

    def project_pool(i, _):
        y = dot(c0[pl.ds(4 * i, 4)].reshape(4 * pwidth, feats), w2t[...])
        wide = (4, pwidth, feats)
        ptop[pl.ds(4 * i, 4)] = y[:, 2 * feats :].astype(BF16).astype(F32).reshape(wide)
        pone[pl.ds(4 * i, 4)] = y[:, feats : 2 * feats].reshape(wide)
        pzero[pl.ds(4 * i, 4)] = y[:, :feats].reshape(wide)
        return 0

    lax.fori_loop(0, (prows + 2 * POOL_UP) // 4, project_pool, 0)

    def pool_middle(e):
        stores = []
        for half in range(halves):
            at_half = (e, slice(None), pl.ds(half * LANES, LANES))
            value = (pone[at_half] + 2.0 * stencil(ptop, pcoefs, e, e, half)).astype(BF16)
            stores += [storing(pmid, at_half, value)]
        return stores

    def pool_grad(e):
        stores = []
        for half in range(halves):
            at_half = (e, slice(None), pl.ds(half * LANES, LANES))
            value = pzero[at_half] - ptop[at_half] + stencil(pmid, pcoefs, e, e, half)
            stores += [storing(pgrad, at_half, value)]
        return stores

    by_rows(2, prows + 2 * POOL_UP - 2, pool_middle)
    by_rows(3, prows + 2 * POOL_UP - 3, pool_grad)

    spread_coefficients(
        edge_coefficients(offsets, inside), stack, turned, coefs, 2, 1, rows + 2 * FINE_UP - 1
    )
    receive(0)
    assemble_all(store_px, px, FINE_UP, px_v, px_h, px_c)

    def fine_one(e):
        stores = []
        for half in range(halves):
            at_half = (e, slice(None), pl.ds(half * LANES, LANES))
            value = stencil(v0, coefs, e, e, half).astype(BF16)
            stores += [storing(t1, at_half, value), storing(v1, at_half, value)]
        return stores

    def fine_two(e):
        stores = []
        for half in range(halves):
            at_half = (e, slice(None), pl.ds(half * LANES, LANES))
            value = 2.0 * stencil(v1, coefs, e, e, half) - v0[at_half]
            stores += [storing(t2, at_half, value)]
        return stores

    by_rows(1, rows + 2 * FINE_UP - 1, fine_one)
    by_rows(2, rows + 2 * FINE_UP - 2, fine_two)

    def pool_matrix(shape, fine_dim, repeat):
        f = lax.broadcasted_iota(jnp.int32, shape, fine_dim)
        p = lax.broadcasted_iota(jnp.int32, shape, 1 - fine_dim)
        f, p = (lax.rem(f, repeat), p) if fine_dim else (f, lax.rem(p, repeat))
        return jnp.where((f == 2 * p - 8) | (f == 2 * p - 7), 0.25, 0.0).astype(BF16)

    gather_pool = pool_matrix((pwidth, 2 * width), 1, width)
    spread_pool = pool_matrix((width, 2 * pwidth), 0, pwidth)

    def activate(i, _):
        e = 2 + 4 * i
        flat = (4 * width, feats)
        a = dot(t0[pl.ds(e, 4)].reshape(flat), w1[0])
        a = a + dot(t1[pl.ds(e, 4)].reshape(flat), w1[1])
        a = a + dot(t2[pl.ds(e, 4)].reshape(flat), w1[2])
        s = jax.nn.sigmoid(a)
        slope[pl.ds(4 * i, 4)] = (s * (1.0 + a * (1.0 - s))).reshape(4, width, feats)
        hidden = a * s
        both = [
            hidden[2 * p * width : (2 * p + 1) * width]
            + hidden[(2 * p + 1) * width : (2 * p + 2) * width]
            for p in (0, 1)
        ]
        value = split_dot(gather_pool, both).astype(BF16)
        for p in (0, 1):
            part = value[:, p * feats : (p + 1) * feats]
            q0[2 + 2 * i + p] = part
            z0[2 + 2 * i + p] = part.astype(F32)
        return 0

    lax.fori_loop(0, (prows + 4) // 2, activate, 0)

    col = lax.broadcasted_iota(jnp.int32, (width, feats), 0)
    own_cols = (col >= RIM) & (col < cols + RIM)

    def act_grad(i, _):
        wide = split_dot(spread_pool, [pgrad[3 + 2 * i], pgrad[4 + 2 * i]])
        for r in range(4):
            value = wide[:, (r // 2) * feats : (r // 2 + 1) * feats] * slope[4 * i + 2 + r]
            ag[4 * i + r] = value.astype(BF16)
            agm[4 * i + r] = jnp.where(own_cols, value, 0.0).astype(BF16)
        return 0

    lax.fori_loop(0, (prows + 2) // 2, act_grad, 0)

    def pool_one(e):
        stores = []
        for half in range(halves):
            at_half = (e, slice(None), pl.ds(half * LANES, LANES))
            value = stencil(z0, pcoefs, e, e, half).astype(BF16)
            stores += [storing(q1, at_half, value), storing(z1, at_half, value)]
        return stores

    def pool_two(e):
        stores = []
        for half in range(halves):
            at_half = (e, slice(None), pl.ds(half * LANES, LANES))
            value = 2.0 * stencil(z1, pcoefs, e, e, half) - z0[at_half]
            stores += [storing(q2, at_half, value)]
        return stores

    batch = sums.shape[0] // 2
    half_rows = batch // 2
    block_rows = half_rows // groups
    parts = 3 * feats * halves

    def at(start, size):
        return pl.ds(pl.multiple_of(start, 16), size)

    numbers = iter(range(sum_send.shape[0]))

    def send(source, target, peer):
        number = next(numbers)
        copy = pltpu.make_async_remote_copy(
            src_ref=source, dst_ref=target, send_sem=sum_send.at[number],
            recv_sem=sum_recv.at[number], device_id=peer, device_id_type=MESH,
        )
        copy.start()
        return copy

    def starts(t):
        base_a = t * batch + core * half_rows
        base_b = base_a + quad * block_rows
        return base_a, base_b, base_b + line * chunk

    def patch_sums(t, terms, first, count, back):
        if batch > parts:
            rest = batch - parts
            sb[pl.ds(t * batch + parts, rest), :] = jnp.zeros((rest, LANES), BF16)
            sums[pl.ds(t * batch + parts, rest), :] = jnp.zeros((rest, LANES), F32)
        for k, term in enumerate(terms):
            x = term[pl.ds(first, count)].reshape(back.shape[1], feats)
            value = dot(back, x)
            for half in range(halves):
                place = pl.ds(t * batch + (half * 3 + k) * feats, feats)
                part = value[:, half * LANES : (half + 1) * LANES]
                sums[place, :] = part
                sb[place, :] = part.astype(BF16)

    def start_a(t):
        other = at(t * batch + (1 - core) * half_rows, half_rows)
        return [send(sb.at[other], in_a.at[t], peer_a)]

    def add(copies, start, size, landed):
        for copy in copies:
            copy.wait()
        own = sums[at(start, size), :]
        for j in range(len(copies)):
            own = own + landed(j).astype(F32)
        return own

    def a_to_b(t, copies):
        base_a, base_b, _ = starts(t)
        own = add(copies, base_a, half_rows, lambda j: in_a[t])
        sums[at(base_a, half_rows), :] = own
        sb[at(base_a, half_rows), :] = own.astype(BF16)
        return [
            send(sb.at[at(base_a + q * block_rows, block_rows)], in_b.at[t, j], peer)
            for j, (q, peer) in enumerate(peers_b)
        ]

    def b_to_c(t, copies):
        _, base_b, _ = starts(t)
        own = add(copies, base_b, block_rows, lambda j: in_b[t, j])
        sums[at(base_b, block_rows), :] = own
        sb[at(base_b, block_rows), :] = own.astype(BF16)
        return [
            send(sb.at[at(base_b + z * chunk, chunk)], in_c.at[t, j], peer)
            for j, (z, peer) in enumerate(peers_c)
        ]

    def c_to_c(t, copies):
        base_c = starts(t)[2]
        full[at(base_c, chunk), :] = add(
            copies, base_c, chunk, lambda j: in_c[t, j]
        ).astype(BF16)
        region = full.at[at(base_c, chunk)]
        return [send(region, region, peer) for _, peer in peers_c]

    def c_to_b(t, copies):
        for copy in copies:
            copy.wait()
        region = full.at[at(starts(t)[1], block_rows)]
        return [send(region, region, peer) for _, peer in peers_b], send(region, region, peer_a)

    def b_to_a(t, copies):
        copies, first = copies
        onward = [first]
        for j, copy in enumerate(copies):
            copy.wait()
            came = lax.rem(quad + groups - 1 - j, groups)
            region = full.at[at(starts(t)[0] + came * block_rows, block_rows)]
            onward.append(send(region, region, peer_a))
        return onward

    turned_back[...] = agm[pl.ds(2, rows)].reshape(rows * width, feats).T
    patch_sums(0, (t0, t1, t2), FINE_UP, rows, turned_back[...])
    fine = start_a(0)

    by_rows(POOL_UP - 1, prows + POOL_UP + 1, pool_one)
    fine = a_to_b(0, fine)
    by_rows(POOL_UP, prows + POOL_UP, pool_two)
    pcol = lax.broadcasted_iota(jnp.int32, (pwidth, feats), 0)
    own_pcols = (pcol >= RIM) & (pcol < pcols + RIM)

    def mask_cot(r, _):
        cm[r] = jnp.where(own_pcols, c0[POOL_UP + r].astype(F32), 0.0).astype(BF16)
        return 0

    lax.fori_loop(0, prows, mask_cot, 0)

    patch_sums(1, (q0, q1, q2), POOL_UP, prows, cm[...].reshape(prows * pwidth, feats).T)
    pool = start_a(1)

    top, one, zero = v0, v1, slope

    def project_fine(i, _):
        y = dot(ag[pl.ds(4 * i, 4)].reshape(4 * width, feats), w1t[...])
        wide = (4, width, feats)
        top[pl.ds(4 * i, 4)] = y[:, 2 * feats :].astype(BF16).astype(F32).reshape(wide)
        one[pl.ds(4 * i, 4)] = y[:, feats : 2 * feats].reshape(wide)
        zero[pl.ds(4 * i, 4)] = y[:, :feats].reshape(wide)
        return 0

    def fine_middle(a):
        stores = []
        for half in range(halves):
            at_half = (a, slice(None), pl.ds(half * LANES, LANES))
            value = (one[at_half] + 2.0 * stencil(top, coefs, a, a + 4, half)).astype(BF16)
            stores += [storing(mid, at_half, value)]
        return stores

    def fine_grad(a):
        stores = []
        for half in range(halves):
            at_half = (a, slice(None), pl.ds(half * LANES, LANES))
            value = zero[at_half] - top[at_half] + stencil(mid, coefs, a, a + 4, half)
            out_half = (a - 2, slice(None), at_half[2])
            stores += [storing(gp, out_half, value[RIM : RIM + cols])]
        return stores

    lax.fori_loop(0, (rows + 4) // 4, project_fine, 0)
    pool = a_to_b(1, pool)
    fine = b_to_c(0, fine)
    by_rows(1, rows + 3, fine_middle)
    fine = c_to_c(0, fine)
    pool = b_to_c(1, pool)
    by_rows(2, rows // 2 + 2, fine_grad)
    fine = c_to_b(0, fine)
    pool = c_to_c(1, pool)
    by_rows(rows // 2 + 2, rows + 2, fine_grad)
    pool = c_to_b(1, pool)

    flat = (prows * pwidth, feats)
    out = dot(q0[pl.ds(POOL_UP, prows)].reshape(flat), w2[0])
    out = out + dot(q1[pl.ds(POOL_UP, prows)].reshape(flat), w2[1])
    out = out + dot(q2[pl.ds(POOL_UP, prows)].reshape(flat), w2[2])
    for r in range(prows):
        start = r * pwidth + RIM
        level[r] = out[start : start + pcols].astype(BF16)

    fine = b_to_a(0, fine)
    pool = b_to_a(1, pool)
    for copy in fine + pool:
        copy.wait()
    for dr, dc, exists, peer in around:
        @pl.when(exists)
        def _():
            for copy in halo_copies(dr, dc, peer)[0]:
                copy().wait_send()


def finish(full_in, gp, level, gp_out, gfirst, gsecond, level_out, full, sems):
    load = pltpu.make_async_copy(full_in, full, sems.at[0])
    pass_pixels = pltpu.make_async_copy(gp, gp_out, sems.at[1])
    pass_level = pltpu.make_async_copy(level, level_out, sems.at[2])
    for copy in (load, pass_pixels, pass_level):
        copy.start()
    load.wait()
    feats = gfirst.shape[1]
    halves = feats // LANES
    batch = full.shape[0] // 2
    count = gfirst.shape[0]
    squares = jnp.zeros((8, LANES), F32)
    for t in range(2):
        x = full[pl.ds(t * batch, count * halves), :].astype(F32)
        squares = squares + jnp.sum((x * x).reshape(count * halves // 8, 8, LANES), axis=0)
    square_sum = jnp.sum(jnp.sum(squares, axis=0, keepdims=True), axis=1, keepdims=True)
    factor = jnp.minimum(1.0, 2.0 * feats * lax.rsqrt(square_sum + 1e-06))
    for t, out in enumerate((gfirst, gsecond)):
        for half in range(halves):
            for k in range(count // feats):
                x = full[pl.ds(t * batch + half * count + k * feats, feats), :].astype(F32)
                out[pl.ds(k * feats + half * LANES, LANES), :] = x.T * factor
    pass_pixels.wait()
    pass_level.wait()


def shards(groups, members, pixels, offsets, first_weights, second_weights, cotangent):
    rows, cols, feats = pixels.shape
    prows, pcols = cotangent.shape[:2]
    width, pwidth = cols + 2 * RIM, pcols + 2 * RIM
    high, phigh, bhigh = rows + 2 * FINE_UP, prows + 2 * POOL_UP, rows + 4
    count = groups * members
    chunk = -(-3 * feats * (feats // LANES) // (count * 16)) * 16
    total = chunk * count
    half = total // 2
    lines = members // 2
    orders = len(STEPS)

    def blocks(n):
        return -(-orders * n // LANES)

    nf, np_ = blocks(rows + 16), blocks(phigh)
    vm = pltpu.VMEM

    def halo(n, up, c):
        return [
            vm((2, n // 2, 16, feats), BF16),
            vm((2, up, c, feats), BF16),
            vm((2, n // 2, 16, feats), BF16),
            vm((4, up // 2, 16, feats), BF16),
        ]

    scratch = [vm((rows, LANES), F32), vm((orders, rows, LANES), F32)]
    scratch += halo(rows, FINE_UP, cols) + halo(prows, POOL_UP, pcols)
    scratch += [
        vm((rows + 16, LANES), F32),
        vm((nf * LANES, LANES), F32), vm((nf, LANES, LANES), F32),
        vm((np_ * LANES, LANES), F32), vm((np_, LANES, LANES), F32),
        vm((orders, high, width, LANES), F32), vm((orders, phigh, pwidth, LANES), F32),
    ]
    scratch += [vm((high, width, feats), t) for t in (BF16, BF16, BF16, F32, F32)]
    scratch += [vm((rows + 8, width, feats), F32)]
    scratch += [vm((phigh, pwidth, feats), BF16), vm((prows, pwidth, feats), BF16)]
    scratch += [vm((phigh, pwidth, feats), t) for t in (BF16,) * 3 + (F32,) * 7]
    scratch += [vm((bhigh, width, feats), t) for t in (BF16, BF16, F32)]
    scratch += [vm((feats, 3 * feats), BF16)] * 2 + [vm((feats, rows * width), BF16)]
    scratch += [
        vm((2 * total, LANES), F32), vm((2 * total, LANES), BF16),
        vm((2, half, LANES), BF16),
        vm((2, groups - 1, half // groups, LANES), BF16),
        vm((2, lines - 1, chunk, LANES), BF16),
    ]
    scratch += [pltpu.SemaphoreType.DMA((3, orders))] * 2
    copies = 2 * (3 * groups + 2 * lines - 3)
    scratch += [pltpu.SemaphoreType.DMA((copies,))] * 2
    held, anywhere = pl.BlockSpec(memory_space=pltpu.VMEM), pl.BlockSpec(memory_space=pl.ANY)
    inner_pixels, full, inner_level = pl.pallas_call(
        functools.partial(kernel, groups, members, chunk),
        out_shape=(
            jax.ShapeDtypeStruct(pixels.shape, BF16),
            jax.ShapeDtypeStruct((2 * total, LANES), BF16),
            jax.ShapeDtypeStruct(cotangent.shape, BF16),
        ),
        in_specs=[held] * 5,
        out_specs=[held] * 3,
        scratch_shapes=scratch,
        compiler_params=pltpu.CompilerParams(
            collective_id=0, has_side_effects=True, vmem_limit_bytes=60 * 1024 * 1024
        ),
    )(pixels, offsets, first_weights, second_weights, cotangent)
    grad_pixels, first, second, level = pl.pallas_call(
        finish,
        out_shape=(
            jax.ShapeDtypeStruct(pixels.shape, BF16),
            jax.ShapeDtypeStruct((3 * feats, feats), F32),
            jax.ShapeDtypeStruct((3 * feats, feats), F32),
            jax.ShapeDtypeStruct(cotangent.shape, BF16),
        ),
        in_specs=[anywhere] * 3,
        out_specs=[anywhere, held, held, anywhere],
        scratch_shapes=[vm((2 * total, LANES), BF16), pltpu.SemaphoreType.DMA((3,))],
        compiler_params=pltpu.CompilerParams(vmem_limit_bytes=60 * 1024 * 1024),
    )(full, inner_pixels, inner_level)
    shape = first_weights.shape
    return grad_pixels, first.reshape(shape), second.reshape(shape), level


def solution(mesh):
    groups, members = mesh.shape["grp"], mesh.shape["dev"]
    return jax.shard_map(
        functools.partial(shards, groups, members),
        mesh=mesh,
        in_specs=(P("grp", "dev", None), P("grp", "dev"), P(), P(), P("grp", "dev", None)),
        out_specs=(P("grp", "dev", None), P(), P(), P("grp", "dev", None)),
        check_vma=False,
    )
```

```python
import functools

import jax
import jax.numpy as jnp
from jax import lax
from jax.experimental import pallas as pl
from jax.experimental.pallas import tpu as pltpu
from jax.sharding import PartitionSpec as P

MESH = pl.DeviceIdType.MESH
F32 = jnp.float32
BF16 = jnp.bfloat16
STEPS = (
    (-1, 0, 1.0),
    (1, 0, 1.0),
    (0, -1, 1.0),
    (0, 1, 1.0),
    (-1, -1, 0.5),
    (-1, 1, 0.5),
    (1, -1, 0.5),
    (1, 1, 0.5),
)
INDEX = {(dr, dc): k for k, (dr, dc, _) in enumerate(STEPS)}
LANES = 128
RIM = 8
FINE_UP = 6
POOL_UP = 4


def edge_coefficients(offsets, inside):
    rows = offsets.shape[0]

    def moved(x, dr, dc):
        if dr:
            x = pltpu.roll(x, (-dr) % rows, 0)
        if dc:
            x = pltpu.roll(x, (-dc) % LANES, 1)
        return x

    weights = []
    degree = jnp.zeros_like(offsets)
    for dr, dc, coupling in STEPS:
        gap = offsets - moved(offsets, dr, dc)
        weight = coupling * inside * moved(inside, dr, dc) * jnp.exp(-gap * gap)
        weights.append(weight)
        degree = degree + weight
    root = lax.rsqrt(jnp.maximum(degree, 1e-30)) * inside
    found = []
    for (dr, dc, _), weight in zip(STEPS, weights):
        value = -root * weight * moved(root, dr, dc)
        if dc:
            value = pltpu.roll(value, dc % LANES, 1)
        found.append(value)
    return found


def spread_coefficients(found, stack, turned, coefs, shift, first, last):
    rows = found[0].shape[0]
    for k, value in enumerate(found):
        stack[pl.ds(k * rows, rows), :] = value
    for b in range(stack.shape[0] // LANES):
        turned[b] = stack[pl.ds(b * LANES, LANES), :].T
    width = coefs.shape[2]
    for k in range(len(STEPS)):
        for e in range(first, last):
            block, lane = divmod(k * rows + e + shift, LANES)
            coefs[k, e] = jnp.broadcast_to(
                turned[block, pl.ds(0, width), pl.ds(lane, 1)], (width, LANES)
            )


def stencil(values, coefs, row, coef_row, half):
    lanes = pl.ds(half * LANES, LANES)
    around = [values[row + dr, :, lanes] for dr in (-1, 0, 1)]
    width = around[0].shape[0]

    def column(dc):
        total = None
        for dr in (-1, 0, 1):
            if (dr, dc) in INDEX:
                term = coefs[INDEX[dr, dc], coef_row] * around[dr + 1]
                total = term if total is None else total + term
        return total

    return pltpu.roll(column(-1), 1, 0) + column(0) + pltpu.roll(column(1), width - 1, 0)


def by_rows(first, last, work):
    def two(i, _):
        e = first + 2 * i
        for store in work(e) + work(e + 1):
            store()
        return 0

    lax.fori_loop(0, (last - first) // 2, two, 0)
    if (last - first) % 2:
        for store in work(last - 1):
            store()


def storing(ref, index, value):
    def store():
        ref[index] = value.astype(ref.dtype)

    return store


def dot(a, b):
    return lax.dot_general(a, b, (((1,), (0,)), ((), ())), preferred_element_type=F32)


def split_dot(matrix, values):
    value = jnp.concatenate(values, axis=1)
    high = value.astype(BF16)
    low = (value - high.astype(F32)).astype(BF16)
    return dot(matrix, jnp.concatenate([high, low], axis=0))


def kernel(
    groups, members, chunk,
    px, off, w1, w2, cot,
    gp, full, level,
    off_own, off_in,
    px_pack, px_v, px_h, px_c,
    ct_pack, ct_v, ct_h, ct_c,
    off_ext, stack, turned, pstack, pturned, coefs, pcoefs,
    t0, t1, t2, v0, v1, slope,
    c0, cm, q0, q1, q2, z0, z1, ptop, pone, pzero, pmid, pgrad,
    ag, agm, mid, w1t, w2t, turned_back,
    sums, sb, in_a, in_b, in_c,
    halo_send, halo_recv, sum_send, sum_recv,
):
    rows, cols, feats = px.shape
    prows, pcols = cot.shape[:2]
    width, pwidth = cols + 2 * RIM, pcols + 2 * RIM
    halves = feats // LANES
    g, d = lax.axis_index("grp"), lax.axis_index("dev")

    around = []
    for dr, dc, _ in STEPS:
        ng, nd = g + dr, d + dc
        exists = (ng >= 0) & (ng < groups) & (nd >= 0) & (nd < members)
        around.append((dr, dc, exists, (ng, nd)))
    core, quad, line = lax.rem(g, 2), (g // 2) * 2 + lax.rem(d, 2), d // 2
    lines = members // 2
    peer_a = (g + 1 - 2 * core, d)
    peers_b, peers_c = [], []
    for j in range(1, groups):
        q = lax.rem(quad + j, groups)
        peers_b.append((q, ((q // 2) * 2 + core, line * 2 + lax.rem(q, 2))))
    for j in range(1, lines):
        z = lax.rem(line + j, lines)
        peers_c.append((z, (g, z * 2 + lax.rem(d, 2))))

    barrier = pltpu.get_barrier_semaphore()
    for dr, dc, exists, peer in around:
        @pl.when(exists)
        def _():
            pl.semaphore_signal(barrier, inc=1, device_id=peer, device_id_type=MESH)
    for peer in [peer_a] + [p for _, p in peers_b] + [p for _, p in peers_c]:
        pl.semaphore_signal(barrier, inc=1, device_id=peer, device_id_type=MESH)

    off_own[...] = jnp.zeros_like(off_own)
    off_own[:, pl.ds(0, cols)] = off[...]
    for source, pack in ((px, px_pack), (cot, ct_pack)):
        edge = source.shape[1]

        def pack_pair(i, _):
            for side, start in ((0, 0), (1, edge - 16)):
                cut = 0 if side == 0 else 8
                parts = [
                    source[2 * i + s, pl.ds(start, 16), :].astype(F32)[cut : cut + 8]
                    for s in (0, 1)
                ]
                pack[side, i] = jnp.concatenate(parts, axis=0).astype(BF16)
            return 0

        lax.fori_loop(0, source.shape[0] // 2, pack_pair, 0)

    greeted = groups + lines - 1
    for dr, dc, exists, peer in around:
        greeted = greeted + jnp.where(exists, 1, 0)
    pl.semaphore_wait(barrier, greeted)

    def halo_copies(dr, dc, peer):
        k, o = INDEX[dr, dc], INDEX[-dr, -dc]
        made = []
        for a, (src, pack, up, v, h, c) in enumerate(
            ((px, px_pack, FINE_UP, px_v, px_h, px_c), (cot, ct_pack, POOL_UP, ct_v, ct_h, ct_c))
        ):
            n = src.shape[0]
            if dc == 0:
                source = src.at[pl.ds(0 if dr < 0 else n - up, up)]
                land, here = v.at[o], v.at[k]
            elif dr == 0:
                source = pack.at[0 if dc < 0 else 1]
                land, here = h.at[o - 2], h.at[k - 2]
            else:
                tiles = up // 2
                source = pack.at[
                    0 if dc < 0 else 1, pl.ds(0 if dr < 0 else n // 2 - tiles, tiles)
                ]
                land, here = c.at[o - 4], c.at[k - 4]
            made.append((a, source, land, here))
        made.append((2, off_own, off_in.at[o], off_in.at[k]))
        outgoing, incoming = [], []
        for a, source, land, here in made:
            copy = functools.partial(
                pltpu.make_async_remote_copy, src_ref=source, send_sem=halo_send.at[a, k],
                device_id=peer, device_id_type=MESH,
            )
            outgoing.append(
                functools.partial(copy, dst_ref=land, recv_sem=halo_recv.at[a, o])
            )
            incoming.append(
                (here, functools.partial(copy, dst_ref=here, recv_sem=halo_recv.at[a, k]))
            )
        return outgoing, incoming

    for a in (2, 1, 0):
        for dr, dc, exists, peer in around:
            @pl.when(exists)
            def _():
                halo_copies(dr, dc, peer)[0][a]().start()

    for dr, dc, exists, peer in around:
        @pl.when(jnp.logical_not(exists))
        def _():
            for here, _ in halo_copies(dr, dc, peer)[1]:
                here[...] = jnp.zeros(here.shape, here.dtype)

    def receive(a):
        for dr, dc, exists, peer in around:
            @pl.when(exists)
            def _():
                halo_copies(dr, dc, peer)[1][a][1]().wait_recv()

    for source, target in ((w2, w2t), (w1, w1t)):
        for k in range(source.shape[0]):
            target[:, pl.ds(k * feats, feats)] = source[k].T
    receive(2)

    def lay(left, own, right):
        lane = lax.broadcasted_iota(jnp.int32, own.shape, 1)
        out = jnp.where(lane < RIM, pltpu.roll(left, (RIM - cols) % LANES, 1), 0.0)
        out = jnp.where((lane >= RIM) & (lane < cols + RIM), pltpu.roll(own, RIM, 1), out)
        return jnp.where(
            (lane >= cols + RIM) & (lane < width), pltpu.roll(right, cols + RIM, 1), out
        )

    def slot(dr, dc, cut):
        return off_in[INDEX[dr, dc], cut, :]

    high, low = pl.ds(rows - 8, 8), pl.ds(0, 8)
    off_ext[pl.ds(0, 8), :] = lay(slot(-1, -1, high), slot(-1, 0, high), slot(-1, 1, high))
    off_ext[pl.ds(8, rows), :] = lay(off_in[INDEX[0, -1]], off_own[...], off_in[INDEX[0, 1]])
    off_ext[pl.ds(8 + rows, 8), :] = lay(slot(1, -1, low), slot(1, 0, low), slot(1, 1, low))

    def within(shape, row_start, col_start, row_end, col_end, used):
        r = lax.broadcasted_iota(jnp.int32, shape, 0) + row_start
        lane = lax.broadcasted_iota(jnp.int32, shape, 1)
        c = lane + col_start
        ok = (r >= 0) & (r < row_end) & (c >= 0) & (c < col_end) & (lane < used)
        return jnp.where(ok, 1.0, 0.0).astype(F32)

    offsets = off_ext[...]
    inside = within(
        offsets.shape, g * rows - 8, d * cols - RIM, groups * rows, members * cols, width
    )
    pshape = (prows + 2 * POOL_UP, LANES)
    a_r = lax.broadcasted_iota(jnp.int32, (pshape[0], rows + 16), 0)
    a_f = lax.broadcasted_iota(jnp.int32, (pshape[0], rows + 16), 1)
    by_row = jnp.where((a_f == 2 * a_r) | (a_f == 2 * a_r + 1), 0.5, 0.0).astype(F32)
    b_f = lax.broadcasted_iota(jnp.int32, (LANES, LANES), 0)
    b_l = lax.broadcasted_iota(jnp.int32, (LANES, LANES), 1)
    by_col = jnp.where((b_f == 2 * b_l - 8) | (b_f == 2 * b_l - 7), 0.5, 0.0).astype(F32)
    exact = functools.partial(
        jnp.dot, precision=lax.Precision.HIGHEST, preferred_element_type=F32
    )
    poffsets = exact(exact(by_row, offsets), by_col)
    pinside = within(
        pshape, g * prows - POOL_UP, d * pcols - RIM, groups * prows, members * pcols, pwidth
    )
    spread_coefficients(
        edge_coefficients(poffsets, pinside), pstack, pturned, pcoefs, 0, 1,
        prows + 2 * POOL_UP - 1,
    )

    def assemble(store, start, pairs, middle, left, right):
        def pair(i, _):
            lt, rt = left(i).astype(F32), right(i).astype(F32)
            for s in (0, 1):
                row = jnp.concatenate(
                    [
                        lt[8 * s : 8 * s + 8],
                        middle(2 * i + s).astype(F32),
                        rt[8 * s : 8 * s + 8],
                    ],
                    axis=0,
                )
                store(start + 2 * i + s, row)
            return 0

        lax.fori_loop(0, pairs, pair, 0)

    def store_px(e, row):
        v0[e] = row
        t0[e] = row.astype(BF16)

    def store_cot(e, row):
        c0[e] = row.astype(BF16)

    def assemble_all(store, src, up, v, h, c):
        n = src.shape[0]
        assemble(store, 0, up // 2, lambda r: v[0, r], lambda i: c[0, i], lambda i: c[1, i])
        assemble(store, up, n // 2, lambda r: src[r], lambda i: h[0, i], lambda i: h[1, i])
        assemble(store, up + n, up // 2, lambda r: v[1, r], lambda i: c[2, i], lambda i: c[3, i])

    receive(1)
    assemble_all(store_cot, cot, POOL_UP, ct_v, ct_h, ct_c)

    def project_pool(i, _):
        y = dot(c0[pl.ds(4 * i, 4)].reshape(4 * pwidth, feats), w2t[...])
        wide = (4, pwidth, feats)
        ptop[pl.ds(4 * i, 4)] = y[:, 2 * feats :].astype(BF16).astype(F32).reshape(wide)
        pone[pl.ds(4 * i, 4)] = y[:, feats : 2 * feats].reshape(wide)
        pzero[pl.ds(4 * i, 4)] = y[:, :feats].reshape(wide)
        return 0

    lax.fori_loop(0, (prows + 2 * POOL_UP) // 4, project_pool, 0)

    def pool_middle(e):
        stores = []
        for half in range(halves):
            at_half = (e, slice(None), pl.ds(half * LANES, LANES))
            value = (pone[at_half] + 2.0 * stencil(ptop, pcoefs, e, e, half)).astype(BF16)
            stores += [storing(pmid, at_half, value)]
        return stores

    def pool_grad(e):
        stores = []
        for half in range(halves):
            at_half = (e, slice(None), pl.ds(half * LANES, LANES))
            value = pzero[at_half] - ptop[at_half] + stencil(pmid, pcoefs, e, e, half)
            stores += [storing(pgrad, at_half, value)]
        return stores

    by_rows(2, prows + 2 * POOL_UP - 2, pool_middle)
    by_rows(3, prows + 2 * POOL_UP - 3, pool_grad)

    spread_coefficients(
        edge_coefficients(offsets, inside), stack, turned, coefs, 2, 1, rows + 2 * FINE_UP - 1
    )
    receive(0)
    assemble_all(store_px, px, FINE_UP, px_v, px_h, px_c)

    def fine_one(e):
        stores = []
        for half in range(halves):
            at_half = (e, slice(None), pl.ds(half * LANES, LANES))
            value = stencil(v0, coefs, e, e, half).astype(BF16)
            stores += [storing(t1, at_half, value), storing(v1, at_half, value)]
        return stores

    def fine_two(e):
        stores = []
        for half in range(halves):
            at_half = (e, slice(None), pl.ds(half * LANES, LANES))
            value = 2.0 * stencil(v1, coefs, e, e, half) - v0[at_half]
            stores += [storing(t2, at_half, value)]
        return stores

    by_rows(FINE_UP - 1, rows + FINE_UP + 1, fine_one)
    by_rows(FINE_UP, rows + FINE_UP, fine_two)

    def pool_matrix(shape, fine_dim, repeat):
        f = lax.broadcasted_iota(jnp.int32, shape, fine_dim)
        p = lax.broadcasted_iota(jnp.int32, shape, 1 - fine_dim)
        f, p = (lax.rem(f, repeat), p) if fine_dim else (f, lax.rem(p, repeat))
        return jnp.where((f == 2 * p - 8) | (f == 2 * p - 7), 0.25, 0.0).astype(BF16)

    gather_pool = pool_matrix((pwidth, 2 * width), 1, width)
    spread_pool = pool_matrix((width, 2 * pwidth), 0, pwidth)

    def activate(i, _):
        e = 2 + 4 * i
        flat = (4 * width, feats)
        a = dot(t0[pl.ds(e, 4)].reshape(flat), w1[0])
        a = a + dot(t1[pl.ds(e, 4)].reshape(flat), w1[1])
        a = a + dot(t2[pl.ds(e, 4)].reshape(flat), w1[2])
        s = jax.nn.sigmoid(a)
        slope[pl.ds(4 * i, 4)] = (s * (1.0 + a * (1.0 - s))).reshape(4, width, feats)
        hidden = a * s
        both = [
            hidden[2 * p * width : (2 * p + 1) * width]
            + hidden[(2 * p + 1) * width : (2 * p + 2) * width]
            for p in (0, 1)
        ]
        value = split_dot(gather_pool, both).astype(BF16)
        for p in (0, 1):
            part = value[:, p * feats : (p + 1) * feats]
            q0[2 + 2 * i + p] = part
            z0[2 + 2 * i + p] = part.astype(F32)
        return 0

    lax.fori_loop(1, prows // 2 + 1, activate, 0)

    col = lax.broadcasted_iota(jnp.int32, (width, feats), 0)
    own_cols = (col >= RIM) & (col < cols + RIM)

    def act_pair(blocks, masked):
        wide = split_dot(spread_pool, [pgrad[POOL_UP + p] for p in blocks])
        for b, p in enumerate(blocks):
            for r in (0, 1):
                value = wide[:, b * feats : (b + 1) * feats] * slope[2 * p + 4 + r]
                ag[2 * p + 2 + r] = value.astype(BF16)
                if masked:
                    agm[2 * p + r] = jnp.where(own_cols, value, 0.0).astype(BF16)

    def act_grad(i, _):
        act_pair((2 * i, 2 * i + 1), True)
        return 0

    lax.fori_loop(0, prows // 2, act_grad, 0)

    def pool_one(e):
        stores = []
        for half in range(halves):
            at_half = (e, slice(None), pl.ds(half * LANES, LANES))
            value = stencil(z0, pcoefs, e, e, half).astype(BF16)
            stores += [storing(q1, at_half, value), storing(z1, at_half, value)]
        return stores

    def pool_two(e):
        stores = []
        for half in range(halves):
            at_half = (e, slice(None), pl.ds(half * LANES, LANES))
            value = 2.0 * stencil(z1, pcoefs, e, e, half) - z0[at_half]
            stores += [storing(q2, at_half, value)]
        return stores

    batch = sums.shape[0] // 2
    half_rows = batch // 2
    block_rows = half_rows // groups
    parts = 3 * feats * halves

    def at(start, size):
        return pl.ds(pl.multiple_of(start, 16), size)

    numbers = iter(range(sum_send.shape[0]))

    def send(source, target, peer):
        number = next(numbers)
        copy = pltpu.make_async_remote_copy(
            src_ref=source, dst_ref=target, send_sem=sum_send.at[number],
            recv_sem=sum_recv.at[number], device_id=peer, device_id_type=MESH,
        )
        copy.start()
        return copy

    def starts(t):
        base_a = t * batch + core * half_rows
        base_b = base_a + quad * block_rows
        return base_a, base_b, base_b + line * chunk

    def patch_sums(t, terms, first, count, back):
        if batch > parts:
            rest = batch - parts
            sb[pl.ds(t * batch + parts, rest), :] = jnp.zeros((rest, LANES), BF16)
            sums[pl.ds(t * batch + parts, rest), :] = jnp.zeros((rest, LANES), F32)
        for k, term in enumerate(terms):
            x = term[pl.ds(first, count)].reshape(back.shape[1], feats)
            value = dot(back, x)
            for half in range(halves):
                place = pl.ds(t * batch + (half * 3 + k) * feats, feats)
                part = value[:, half * LANES : (half + 1) * LANES]
                sums[place, :] = part
                sb[place, :] = part.astype(BF16)

    def start_a(t):
        other = at(t * batch + (1 - core) * half_rows, half_rows)
        return [send(sb.at[other], in_a.at[t], peer_a)]

    def add(copies, start, size, landed):
        for copy in copies:
            copy.wait()
        own = sums[at(start, size), :]
        for j in range(len(copies)):
            own = own + landed(j).astype(F32)
        return own

    def a_to_b(t, copies):
        base_a, base_b, _ = starts(t)
        own = add(copies, base_a, half_rows, lambda j: in_a[t])
        sums[at(base_a, half_rows), :] = own
        sb[at(base_a, half_rows), :] = own.astype(BF16)
        return [
            send(sb.at[at(base_a + q * block_rows, block_rows)], in_b.at[t, j], peer)
            for j, (q, peer) in enumerate(peers_b)
        ]

    def b_to_c(t, copies):
        _, base_b, _ = starts(t)
        own = add(copies, base_b, block_rows, lambda j: in_b[t, j])
        sums[at(base_b, block_rows), :] = own
        sb[at(base_b, block_rows), :] = own.astype(BF16)
        return [
            send(sb.at[at(base_b + z * chunk, chunk)], in_c.at[t, j], peer)
            for j, (z, peer) in enumerate(peers_c)
        ]

    def c_to_c(t, copies):
        base_c = starts(t)[2]
        full[at(base_c, chunk), :] = add(
            copies, base_c, chunk, lambda j: in_c[t, j]
        ).astype(BF16)
        region = full.at[at(base_c, chunk)]
        return [send(region, region, peer) for _, peer in peers_c]

    def c_to_b(t, copies):
        for copy in copies:
            copy.wait()
        region = full.at[at(starts(t)[1], block_rows)]
        return [send(region, region, peer) for _, peer in peers_b], send(region, region, peer_a)

    def b_to_a(t, copies):
        copies, first = copies
        onward = [first]
        for j, copy in enumerate(copies):
            copy.wait()
            came = lax.rem(quad + groups - 1 - j, groups)
            region = full.at[at(starts(t)[0] + came * block_rows, block_rows)]
            onward.append(send(region, region, peer_a))
        return onward

    turned_back[...] = agm[...].reshape(rows * width, feats).T
    patch_sums(0, (t0, t1, t2), FINE_UP, rows, turned_back[...])
    fine = start_a(0)

    by_rows(1, FINE_UP - 1, fine_one)
    by_rows(rows + FINE_UP + 1, rows + 2 * FINE_UP - 1, fine_one)
    by_rows(2, FINE_UP, fine_two)
    by_rows(rows + FINE_UP, rows + 2 * FINE_UP - 2, fine_two)
    fine = a_to_b(0, fine)
    lax.fori_loop(0, 2, lambda j, c: activate(j * (prows // 2 + 1), c), 0)
    act_pair((-1, prows), False)
    by_rows(POOL_UP - 1, prows + POOL_UP + 1, pool_one)
    by_rows(POOL_UP, prows + POOL_UP, pool_two)
    fine = b_to_c(0, fine)

    pcol = lax.broadcasted_iota(jnp.int32, (pwidth, feats), 0)
    own_pcols = (pcol >= RIM) & (pcol < pcols + RIM)

    def mask_cot(r, _):
        cm[r] = jnp.where(own_pcols, c0[POOL_UP + r].astype(F32), 0.0).astype(BF16)
        return 0

    lax.fori_loop(0, prows, mask_cot, 0)

    patch_sums(1, (q0, q1, q2), POOL_UP, prows, cm[...].reshape(prows * pwidth, feats).T)
    pool = start_a(1)

    top, one, zero = v0, v1, slope

    def project_fine(i, _):
        y = dot(ag[pl.ds(4 * i, 4)].reshape(4 * width, feats), w1t[...])
        wide = (4, width, feats)
        top[pl.ds(4 * i, 4)] = y[:, 2 * feats :].astype(BF16).astype(F32).reshape(wide)
        one[pl.ds(4 * i, 4)] = y[:, feats : 2 * feats].reshape(wide)
        zero[pl.ds(4 * i, 4)] = y[:, :feats].reshape(wide)
        return 0

    def fine_middle(a):
        stores = []
        for half in range(halves):
            at_half = (a, slice(None), pl.ds(half * LANES, LANES))
            value = (one[at_half] + 2.0 * stencil(top, coefs, a, a + 4, half)).astype(BF16)
            stores += [storing(mid, at_half, value)]
        return stores

    def fine_grad(a):
        stores = []
        for half in range(halves):
            at_half = (a, slice(None), pl.ds(half * LANES, LANES))
            value = zero[at_half] - top[at_half] + stencil(mid, coefs, a, a + 4, half)
            out_half = (a - 2, slice(None), at_half[2])
            stores += [storing(gp, out_half, value[RIM : RIM + cols])]
        return stores

    lax.fori_loop(0, (rows + 4) // 4, project_fine, 0)
    fine = c_to_c(0, fine)
    pool = a_to_b(1, pool)
    by_rows(1, rows + 3, fine_middle)
    fine = c_to_b(0, fine)
    pool = b_to_c(1, pool)
    by_rows(2, rows // 2 + 2, fine_grad)
    pool = c_to_c(1, pool)
    by_rows(rows // 2 + 2, rows + 2, fine_grad)
    fine = b_to_a(0, fine)
    pool = c_to_b(1, pool)

    flat = (prows * pwidth, feats)
    out = dot(q0[pl.ds(POOL_UP, prows)].reshape(flat), w2[0])
    out = out + dot(q1[pl.ds(POOL_UP, prows)].reshape(flat), w2[1])
    out = out + dot(q2[pl.ds(POOL_UP, prows)].reshape(flat), w2[2])
    for r in range(prows):
        start = r * pwidth + RIM
        level[r] = out[start : start + pcols].astype(BF16)

    pool = b_to_a(1, pool)
    for copy in fine + pool:
        copy.wait()
    for dr, dc, exists, peer in around:
        @pl.when(exists)
        def _():
            for copy in halo_copies(dr, dc, peer)[0]:
                copy().wait_send()


def finish(
    full_in, gp, level, gp_out, gfirst, gsecond, level_out, full, gp_held, level_held, sems
):
    load = pltpu.make_async_copy(full_in, full, sems.at[0])
    load_pixels = pltpu.make_async_copy(gp, gp_held, sems.at[1])
    load_level = pltpu.make_async_copy(level, level_held, sems.at[2])
    pass_pixels = pltpu.make_async_copy(gp_held, gp_out, sems.at[3])
    pass_level = pltpu.make_async_copy(level_held, level_out, sems.at[4])
    for copy in (load, load_pixels, load_level):
        copy.start()
    load_pixels.wait()
    pass_pixels.start()
    load_level.wait()
    pass_level.start()
    load.wait()
    feats = gfirst.shape[1]
    halves = feats // LANES
    batch = full.shape[0] // 2
    count = gfirst.shape[0]
    squares = jnp.zeros((8, LANES), F32)
    for t in range(2):
        x = full[pl.ds(t * batch, count * halves), :].astype(F32)
        squares = squares + jnp.sum((x * x).reshape(count * halves // 8, 8, LANES), axis=0)
    square_sum = jnp.sum(jnp.sum(squares, axis=0, keepdims=True), axis=1, keepdims=True)
    factor = jnp.minimum(1.0, 2.0 * feats * lax.rsqrt(square_sum + 1e-06))
    for t, out in enumerate((gfirst, gsecond)):
        for half in range(halves):
            for k in range(count // feats):
                x = full[pl.ds(t * batch + half * count + k * feats, feats), :].astype(F32)
                out[pl.ds(k * feats + half * LANES, LANES), :] = x.T * factor
    pass_pixels.wait()
    pass_level.wait()


def shards(groups, members, pixels, offsets, first_weights, second_weights, cotangent):
    rows, cols, feats = pixels.shape
    prows, pcols = cotangent.shape[:2]
    width, pwidth = cols + 2 * RIM, pcols + 2 * RIM
    high, phigh, bhigh = rows + 2 * FINE_UP, prows + 2 * POOL_UP, rows + 4
    count = groups * members
    chunk = -(-3 * feats * (feats // LANES) // (count * 16)) * 16
    total = chunk * count
    half = total // 2
    lines = members // 2
    orders = len(STEPS)

    def blocks(n):
        return -(-orders * n // LANES)

    nf, np_ = blocks(rows + 16), blocks(phigh)
    vm = pltpu.VMEM

    def halo(n, up, c):
        return [
            vm((2, n // 2, 16, feats), BF16),
            vm((2, up, c, feats), BF16),
            vm((2, n // 2, 16, feats), BF16),
            vm((4, up // 2, 16, feats), BF16),
        ]

    scratch = [vm((rows, LANES), F32), vm((orders, rows, LANES), F32)]
    scratch += halo(rows, FINE_UP, cols) + halo(prows, POOL_UP, pcols)
    scratch += [
        vm((rows + 16, LANES), F32),
        vm((nf * LANES, LANES), F32), vm((nf, LANES, LANES), F32),
        vm((np_ * LANES, LANES), F32), vm((np_, LANES, LANES), F32),
        vm((orders, high, width, LANES), F32), vm((orders, phigh, pwidth, LANES), F32),
    ]
    scratch += [vm((high, width, feats), t) for t in (BF16, BF16, BF16, F32, F32)]
    scratch += [vm((rows + 8, width, feats), F32)]
    scratch += [vm((phigh, pwidth, feats), BF16), vm((prows, pwidth, feats), BF16)]
    scratch += [vm((phigh, pwidth, feats), t) for t in (BF16,) * 3 + (F32,) * 7]
    scratch += [vm((n, width, feats), t) for n, t in ((bhigh, BF16), (rows, BF16), (bhigh, F32))]
    scratch += [vm((feats, 3 * feats), BF16)] * 2 + [vm((feats, rows * width), BF16)]
    scratch += [
        vm((2 * total, LANES), F32), vm((2 * total, LANES), BF16),
        vm((2, half, LANES), BF16),
        vm((2, groups - 1, half // groups, LANES), BF16),
        vm((2, lines - 1, chunk, LANES), BF16),
    ]
    scratch += [pltpu.SemaphoreType.DMA((3, orders))] * 2
    copies = 2 * (3 * groups + 2 * lines - 3)
    scratch += [pltpu.SemaphoreType.DMA((copies,))] * 2
    held, anywhere = pl.BlockSpec(memory_space=pltpu.VMEM), pl.BlockSpec(memory_space=pl.ANY)
    inner_pixels, full, inner_level = pl.pallas_call(
        functools.partial(kernel, groups, members, chunk),
        out_shape=(
            jax.ShapeDtypeStruct(pixels.shape, BF16),
            jax.ShapeDtypeStruct((2 * total, LANES), BF16),
            jax.ShapeDtypeStruct(cotangent.shape, BF16),
        ),
        in_specs=[held] * 5,
        out_specs=[held] * 3,
        scratch_shapes=scratch,
        compiler_params=pltpu.CompilerParams(
            collective_id=0, has_side_effects=True, vmem_limit_bytes=60 * 1024 * 1024
        ),
    )(pixels, offsets, first_weights, second_weights, cotangent)
    grad_pixels, first, second, level = pl.pallas_call(
        finish,
        out_shape=(
            jax.ShapeDtypeStruct(pixels.shape, BF16),
            jax.ShapeDtypeStruct((3 * feats, feats), F32),
            jax.ShapeDtypeStruct((3 * feats, feats), F32),
            jax.ShapeDtypeStruct(cotangent.shape, BF16),
        ),
        in_specs=[anywhere] * 3,
        out_specs=[anywhere, held, held, anywhere],
        scratch_shapes=[
            vm((2 * total, LANES), BF16), vm(pixels.shape, BF16), vm(cotangent.shape, BF16),
            pltpu.SemaphoreType.DMA((5,)),
        ],
        compiler_params=pltpu.CompilerParams(vmem_limit_bytes=60 * 1024 * 1024),
    )(full, inner_pixels, inner_level)
    shape = first_weights.shape
    return grad_pixels, first.reshape(shape), second.reshape(shape), level


def solution(mesh):
    groups, members = mesh.shape["grp"], mesh.shape["dev"]
    return jax.shard_map(
        functools.partial(shards, groups, members),
        mesh=mesh,
        in_specs=(P("grp", "dev", None), P("grp", "dev"), P(), P(), P("grp", "dev", None)),
        out_specs=(P("grp", "dev", None), P(), P(), P("grp", "dev", None)),
        check_vma=False,
    )
```

```python
import functools

import jax
import jax.numpy as jnp
from jax import lax
from jax.experimental import pallas as pl
from jax.experimental.pallas import tpu as pltpu
from jax.sharding import PartitionSpec as P

MESH = pl.DeviceIdType.MESH
F32 = jnp.float32
BF16 = jnp.bfloat16
STEPS = (
    (-1, 0, 1.0),
    (1, 0, 1.0),
    (0, -1, 1.0),
    (0, 1, 1.0),
    (-1, -1, 0.5),
    (-1, 1, 0.5),
    (1, -1, 0.5),
    (1, 1, 0.5),
)
INDEX = {(dr, dc): k for k, (dr, dc, _) in enumerate(STEPS)}
LANES = 128
RIM = 8
FINE_UP = 6
POOL_UP = 4


def edge_coefficients(offsets, inside):
    rows = offsets.shape[0]

    def moved(x, dr, dc):
        if dr:
            x = pltpu.roll(x, (-dr) % rows, 0)
        if dc:
            x = pltpu.roll(x, (-dc) % LANES, 1)
        return x

    weights = []
    degree = jnp.zeros_like(offsets)
    for dr, dc, coupling in STEPS:
        gap = offsets - moved(offsets, dr, dc)
        weight = coupling * inside * moved(inside, dr, dc) * jnp.exp(-gap * gap)
        weights.append(weight)
        degree = degree + weight
    root = lax.rsqrt(jnp.maximum(degree, 1e-30)) * inside
    found = []
    for (dr, dc, _), weight in zip(STEPS, weights):
        value = -root * weight * moved(root, dr, dc)
        if dc:
            value = pltpu.roll(value, dc % LANES, 1)
        found.append(value)
    return found


def spread_coefficients(found, stack, turned, coefs, shift, first, last):
    rows = found[0].shape[0]
    for k, value in enumerate(found):
        stack[pl.ds(k * rows, rows), :] = value
    for b in range(stack.shape[0] // LANES):
        turned[b] = stack[pl.ds(b * LANES, LANES), :].T
    width = coefs.shape[2]
    for k, step in enumerate(STEPS):
        if step[:2] == (1, 0):
            continue
        for e in range(first, last):
            block, lane = divmod(k * rows + e + shift, LANES)
            coefs[k, e] = jnp.broadcast_to(
                turned[block, pl.ds(0, width), pl.ds(lane, 1)], (width, LANES)
            )


def stencil(values, coefs, row, coef_row, emit, lead=0):
    tiles = values.shape[1] // 8
    halves = values.shape[2] // LANES
    line = lax.broadcasted_iota(jnp.int32, (8, LANES), 0)
    first, last = line == 0, line == 7
    before = [None] * halves
    done = [[] for _ in range(halves)]

    def close(half, left, centre, right, after):
        done[half].append(left + centre + jnp.where(last, after, right))
        j = len(done[half]) - 1
        if j > lead and (j - lead) % 2:
            emit(8 * (j - 1), half, jnp.concatenate(done[half][-2:], axis=0))

    for j in range(tiles):
        cols = pl.ds(8 * j, 8)
        weight = {
            (dr, dc): coefs[k, coef_row, cols]
            for (dr, dc), k in INDEX.items()
            if (dr, dc) != (1, 0)
        }
        weight[1, 0] = coefs[INDEX[-1, 0], coef_row + 1, cols]
        for half in range(halves):
            up, centre, down = (
                values[row + dr, cols, pl.ds(half * LANES, LANES)] for dr in (-1, 0, 1)
            )
            to_right = weight[-1, -1] * up + weight[0, -1] * centre + weight[1, -1] * down
            to_left = weight[-1, 1] * up + weight[0, 1] * centre + weight[1, 1] * down
            straight = weight[-1, 0] * up + weight[1, 0] * down
            to_right = pltpu.roll(to_right, 1, 0)
            to_left = pltpu.roll(to_left, 7, 0)
            left = to_right
            if j:
                old_right, old_left, old_straight, old_to_left = before[half]
                left = jnp.where(first, old_right, to_right)
                close(half, old_left, old_straight, old_to_left, to_left)
            before[half] = (to_right, left, straight, to_left)
    for half in range(halves):
        _, left, straight, to_left = before[half]
        close(half, left, straight, to_left, to_left)


def by_rows(first, last, work):
    def two(i, _):
        work(first + 2 * i)
        work(first + 2 * i + 1)
        return 0

    lax.fori_loop(0, (last - first) // 2, two, 0)
    if (last - first) % 2:
        work(last - 1)


def dot(a, b):
    return lax.dot_general(a, b, (((1,), (0,)), ((), ())), preferred_element_type=F32)


def split_dot(matrix, values):
    value = jnp.concatenate(values, axis=1)
    high = value.astype(BF16)
    low = (value - high.astype(F32)).astype(BF16)
    return dot(matrix, jnp.concatenate([high, low], axis=0))


def kernel(
    groups, members, chunk,
    px, off, w1, w2, cot,
    gp, full, level,
    off_own, off_in,
    px_pack, px_v, px_h, px_c,
    ct_pack, ct_v, ct_h, ct_c,
    off_ext, stack, turned, pstack, pturned, coefs, pcoefs,
    t0, t1, t2, v0, v1, slope,
    c0, cm, q0, q1, q2, z0, z1, ptop, pone, pzero, pmid, pgrad,
    ag, agm, mid, w1t, w2t, turned_back,
    sums, sb, in_a, in_b, in_c,
    halo_send, halo_recv, sum_send, sum_recv,
):
    rows, cols, feats = px.shape
    prows, pcols = cot.shape[:2]
    width, pwidth = cols + 2 * RIM, pcols + 2 * RIM
    halves = feats // LANES
    g, d = lax.axis_index("grp"), lax.axis_index("dev")

    around = []
    for dr, dc, _ in STEPS:
        ng, nd = g + dr, d + dc
        exists = (ng >= 0) & (ng < groups) & (nd >= 0) & (nd < members)
        around.append((dr, dc, exists, (ng, nd)))
    core, quad, line = lax.rem(g, 2), (g // 2) * 2 + lax.rem(d, 2), d // 2
    lines = members // 2
    peer_a = (g + 1 - 2 * core, d)
    peers_b, peers_c = [], []
    for j in range(1, groups):
        q = lax.rem(quad + j, groups)
        peers_b.append((q, ((q // 2) * 2 + core, line * 2 + lax.rem(q, 2))))
    for j in range(1, lines):
        z = lax.rem(line + j, lines)
        peers_c.append((z, (g, z * 2 + lax.rem(d, 2))))

    barrier = pltpu.get_barrier_semaphore()
    for dr, dc, exists, peer in around:
        @pl.when(exists)
        def _():
            pl.semaphore_signal(barrier, inc=1, device_id=peer, device_id_type=MESH)
    for peer in [peer_a] + [p for _, p in peers_b] + [p for _, p in peers_c]:
        pl.semaphore_signal(barrier, inc=1, device_id=peer, device_id_type=MESH)

    off_own[...] = jnp.zeros_like(off_own)
    off_own[:, pl.ds(0, cols)] = off[...]
    for source, pack in ((px, px_pack), (cot, ct_pack)):
        edge = source.shape[1]

        def pack_pair(i, _):
            for side, start in ((0, 0), (1, edge - 16)):
                cut = 0 if side == 0 else 8
                parts = [
                    source[2 * i + s, pl.ds(start, 16), :].astype(F32)[cut : cut + 8]
                    for s in (0, 1)
                ]
                pack[side, i] = jnp.concatenate(parts, axis=0).astype(BF16)
            return 0

        lax.fori_loop(0, source.shape[0] // 2, pack_pair, 0)

    greeted = groups + lines - 1
    for dr, dc, exists, peer in around:
        greeted = greeted + jnp.where(exists, 1, 0)
    pl.semaphore_wait(barrier, greeted)

    def halo_copies(dr, dc, peer):
        k, o = INDEX[dr, dc], INDEX[-dr, -dc]
        made = []
        for a, (src, pack, up, v, h, c) in enumerate(
            ((px, px_pack, FINE_UP, px_v, px_h, px_c), (cot, ct_pack, POOL_UP, ct_v, ct_h, ct_c))
        ):
            n = src.shape[0]
            if dc == 0:
                source = src.at[pl.ds(0 if dr < 0 else n - up, up)]
                land, here = v.at[o], v.at[k]
            elif dr == 0:
                source = pack.at[0 if dc < 0 else 1]
                land, here = h.at[o - 2], h.at[k - 2]
            else:
                tiles = up // 2
                source = pack.at[
                    0 if dc < 0 else 1, pl.ds(0 if dr < 0 else n // 2 - tiles, tiles)
                ]
                land, here = c.at[o - 4], c.at[k - 4]
            made.append((a, source, land, here))
        made.append((2, off_own, off_in.at[o], off_in.at[k]))
        outgoing, incoming = [], []
        for a, source, land, here in made:
            copy = functools.partial(
                pltpu.make_async_remote_copy, src_ref=source, send_sem=halo_send.at[a, k],
                device_id=peer, device_id_type=MESH,
            )
            outgoing.append(
                functools.partial(copy, dst_ref=land, recv_sem=halo_recv.at[a, o])
            )
            incoming.append(
                (here, functools.partial(copy, dst_ref=here, recv_sem=halo_recv.at[a, k]))
            )
        return outgoing, incoming

    for a in (2, 1, 0):
        for dr, dc, exists, peer in around:
            @pl.when(exists)
            def _():
                halo_copies(dr, dc, peer)[0][a]().start()

    for dr, dc, exists, peer in around:
        @pl.when(jnp.logical_not(exists))
        def _():
            for here, _ in halo_copies(dr, dc, peer)[1]:
                here[...] = jnp.zeros(here.shape, here.dtype)

    def receive(a):
        for dr, dc, exists, peer in around:
            @pl.when(exists)
            def _():
                halo_copies(dr, dc, peer)[1][a][1]().wait_recv()

    for source, target in ((w2, w2t), (w1, w1t)):
        for k in range(source.shape[0]):
            target[:, pl.ds(k * feats, feats)] = source[k].T
    receive(2)

    def lay(left, own, right):
        lane = lax.broadcasted_iota(jnp.int32, own.shape, 1)
        out = jnp.where(lane < RIM, pltpu.roll(left, (RIM - cols) % LANES, 1), 0.0)
        out = jnp.where((lane >= RIM) & (lane < cols + RIM), pltpu.roll(own, RIM, 1), out)
        return jnp.where(
            (lane >= cols + RIM) & (lane < width), pltpu.roll(right, cols + RIM, 1), out
        )

    def slot(dr, dc, cut):
        return off_in[INDEX[dr, dc], cut, :]

    high, low = pl.ds(rows - 8, 8), pl.ds(0, 8)
    off_ext[pl.ds(0, 8), :] = lay(slot(-1, -1, high), slot(-1, 0, high), slot(-1, 1, high))
    off_ext[pl.ds(8, rows), :] = lay(off_in[INDEX[0, -1]], off_own[...], off_in[INDEX[0, 1]])
    off_ext[pl.ds(8 + rows, 8), :] = lay(slot(1, -1, low), slot(1, 0, low), slot(1, 1, low))

    def within(shape, row_start, col_start, row_end, col_end, used):
        r = lax.broadcasted_iota(jnp.int32, shape, 0) + row_start
        lane = lax.broadcasted_iota(jnp.int32, shape, 1)
        c = lane + col_start
        ok = (r >= 0) & (r < row_end) & (c >= 0) & (c < col_end) & (lane < used)
        return jnp.where(ok, 1.0, 0.0).astype(F32)

    offsets = off_ext[...]
    inside = within(
        offsets.shape, g * rows - 8, d * cols - RIM, groups * rows, members * cols, width
    )
    pshape = (prows + 2 * POOL_UP, LANES)
    a_r = lax.broadcasted_iota(jnp.int32, (pshape[0], rows + 16), 0)
    a_f = lax.broadcasted_iota(jnp.int32, (pshape[0], rows + 16), 1)
    by_row = jnp.where((a_f == 2 * a_r) | (a_f == 2 * a_r + 1), 0.5, 0.0).astype(F32)
    b_f = lax.broadcasted_iota(jnp.int32, (LANES, LANES), 0)
    b_l = lax.broadcasted_iota(jnp.int32, (LANES, LANES), 1)
    by_col = jnp.where((b_f == 2 * b_l - 8) | (b_f == 2 * b_l - 7), 0.5, 0.0).astype(F32)
    exact = functools.partial(
        jnp.dot, precision=lax.Precision.HIGHEST, preferred_element_type=F32
    )
    poffsets = exact(exact(by_row, offsets), by_col)
    pinside = within(
        pshape, g * prows - POOL_UP, d * pcols - RIM, groups * prows, members * pcols, pwidth
    )
    spread_coefficients(
        edge_coefficients(poffsets, pinside), pstack, pturned, pcoefs, 0, 1,
        prows + 2 * POOL_UP,
    )

    def assemble(store, start, pairs, middle, left, right):
        def pair(i, _):
            lt, rt = left(i).astype(F32), right(i).astype(F32)
            for s in (0, 1):
                row = jnp.concatenate(
                    [
                        lt[8 * s : 8 * s + 8],
                        middle(2 * i + s).astype(F32),
                        rt[8 * s : 8 * s + 8],
                    ],
                    axis=0,
                )
                store(start + 2 * i + s, row)
            return 0

        lax.fori_loop(0, pairs, pair, 0)

    def store_px(e, row):
        v0[e] = row
        t0[e] = row.astype(BF16)

    def store_cot(e, row):
        c0[e] = row.astype(BF16)

    def assemble_all(store, src, up, v, h, c):
        n = src.shape[0]
        assemble(store, 0, up // 2, lambda r: v[0, r], lambda i: c[0, i], lambda i: c[1, i])
        assemble(store, up, n // 2, lambda r: src[r], lambda i: h[0, i], lambda i: h[1, i])
        assemble(store, up + n, up // 2, lambda r: v[1, r], lambda i: c[2, i], lambda i: c[3, i])

    receive(1)
    assemble_all(store_cot, cot, POOL_UP, ct_v, ct_h, ct_c)

    def project_pool(i, _):
        y = dot(c0[pl.ds(4 * i, 4)].reshape(4 * pwidth, feats), w2t[...])
        wide = (4, pwidth, feats)
        ptop[pl.ds(4 * i, 4)] = y[:, 2 * feats :].astype(BF16).astype(F32).reshape(wide)
        pone[pl.ds(4 * i, 4)] = y[:, feats : 2 * feats].reshape(wide)
        pzero[pl.ds(4 * i, 4)] = y[:, :feats].reshape(wide)
        return 0

    lax.fori_loop(0, (prows + 2 * POOL_UP) // 4, project_pool, 0)

    def pool_middle(e):
        def emit(col, half, value):
            at = (e, pl.ds(col, 16), pl.ds(half * LANES, LANES))
            pmid[at] = (pone[at] + 2.0 * value).astype(BF16).astype(F32)

        stencil(ptop, pcoefs, e, e, emit)

    def pool_grad(e):
        def emit(col, half, value):
            at = (e, pl.ds(col, 16), pl.ds(half * LANES, LANES))
            pgrad[at] = pzero[at] - ptop[at] + value

        stencil(pmid, pcoefs, e, e, emit)

    by_rows(2, prows + 2 * POOL_UP - 2, pool_middle)
    by_rows(3, prows + 2 * POOL_UP - 3, pool_grad)

    spread_coefficients(
        edge_coefficients(offsets, inside), stack, turned, coefs, 2, 1, rows + 2 * FINE_UP
    )
    receive(0)
    assemble_all(store_px, px, FINE_UP, px_v, px_h, px_c)

    def fine_one(e):
        def emit(col, half, value):
            at = (e, pl.ds(col, 16), pl.ds(half * LANES, LANES))
            value = value.astype(BF16)
            t1[at] = value
            v1[at] = value.astype(F32)

        stencil(v0, coefs, e, e, emit)

    def fine_two(e):
        def emit(col, half, value):
            at = (e, pl.ds(col, 16), pl.ds(half * LANES, LANES))
            t2[at] = (2.0 * value - v0[at]).astype(BF16)

        stencil(v1, coefs, e, e, emit)

    by_rows(1, rows + 2 * FINE_UP - 1, fine_one)
    by_rows(2, rows + 2 * FINE_UP - 2, fine_two)

    def pool_matrix(shape, fine_dim, repeat):
        f = lax.broadcasted_iota(jnp.int32, shape, fine_dim)
        p = lax.broadcasted_iota(jnp.int32, shape, 1 - fine_dim)
        f, p = (lax.rem(f, repeat), p) if fine_dim else (f, lax.rem(p, repeat))
        return jnp.where((f == 2 * p - 8) | (f == 2 * p - 7), 0.25, 0.0).astype(BF16)

    gather_pool = pool_matrix((pwidth, 2 * width), 1, width)
    spread_pool = pool_matrix((width, 2 * pwidth), 0, pwidth)

    def activate(i, _):
        e = 2 + 4 * i
        flat = (4 * width, feats)
        a = dot(t0[pl.ds(e, 4)].reshape(flat), w1[0])
        a = a + dot(t1[pl.ds(e, 4)].reshape(flat), w1[1])
        a = a + dot(t2[pl.ds(e, 4)].reshape(flat), w1[2])
        s = jax.nn.sigmoid(a)
        slope[pl.ds(4 * i, 4)] = (s * (1.0 + a * (1.0 - s))).reshape(4, width, feats)
        hidden = a * s
        both = [
            hidden[2 * p * width : (2 * p + 1) * width]
            + hidden[(2 * p + 1) * width : (2 * p + 2) * width]
            for p in (0, 1)
        ]
        value = split_dot(gather_pool, both).astype(BF16)
        for p in (0, 1):
            part = value[:, p * feats : (p + 1) * feats]
            q0[2 + 2 * i + p] = part
            z0[2 + 2 * i + p] = part.astype(F32)
        return 0

    lax.fori_loop(0, (prows + 4) // 2, activate, 0)

    col = lax.broadcasted_iota(jnp.int32, (width, feats), 0)
    own_cols = (col >= RIM) & (col < cols + RIM)

    def act_grad(i, _):
        wide = split_dot(spread_pool, [pgrad[3 + 2 * i], pgrad[4 + 2 * i]])
        for r in range(4):
            value = wide[:, (r // 2) * feats : (r // 2 + 1) * feats] * slope[4 * i + 2 + r]
            ag[4 * i + r] = value.astype(BF16)
            agm[4 * i + r] = jnp.where(own_cols, value, 0.0).astype(BF16)
        return 0

    lax.fori_loop(0, (prows + 2) // 2, act_grad, 0)

    def pool_one(e):
        def emit(col, half, value):
            at = (e, pl.ds(col, 16), pl.ds(half * LANES, LANES))
            value = value.astype(BF16)
            q1[at] = value
            z1[at] = value.astype(F32)

        stencil(z0, pcoefs, e, e, emit)

    def pool_two(e):
        def emit(col, half, value):
            at = (e, pl.ds(col, 16), pl.ds(half * LANES, LANES))
            q2[at] = (2.0 * value - z0[at]).astype(BF16)

        stencil(z1, pcoefs, e, e, emit)

    batch = sums.shape[0] // 2
    half_rows = batch // 2
    block_rows = half_rows // groups
    parts = 3 * feats * halves

    def at(start, size):
        return pl.ds(pl.multiple_of(start, 16), size)

    numbers = iter(range(sum_send.shape[0]))

    def send(source, target, peer):
        number = next(numbers)
        copy = pltpu.make_async_remote_copy(
            src_ref=source, dst_ref=target, send_sem=sum_send.at[number],
            recv_sem=sum_recv.at[number], device_id=peer, device_id_type=MESH,
        )
        copy.start()
        return copy

    def starts(t):
        base_a = t * batch + core * half_rows
        base_b = base_a + quad * block_rows
        return base_a, base_b, base_b + line * chunk

    def patch_sums(t, terms, first, count, back):
        if batch > parts:
            rest = batch - parts
            sb[pl.ds(t * batch + parts, rest), :] = jnp.zeros((rest, LANES), BF16)
            sums[pl.ds(t * batch + parts, rest), :] = jnp.zeros((rest, LANES), F32)
        for k, term in enumerate(terms):
            x = term[pl.ds(first, count)].reshape(back.shape[1], feats)
            value = dot(back, x)
            for half in range(halves):
                place = pl.ds(t * batch + (half * 3 + k) * feats, feats)
                part = value[:, half * LANES : (half + 1) * LANES]
                sums[place, :] = part
                sb[place, :] = part.astype(BF16)

    def start_a(t):
        other = at(t * batch + (1 - core) * half_rows, half_rows)
        return [send(sb.at[other], in_a.at[t], peer_a)]

    def add(copies, start, size, landed):
        for copy in copies:
            copy.wait()
        own = sums[at(start, size), :]
        for j in range(len(copies)):
            own = own + landed(j).astype(F32)
        return own

    def a_to_b(t, copies):
        base_a, base_b, _ = starts(t)
        own = add(copies, base_a, half_rows, lambda j: in_a[t])
        sums[at(base_a, half_rows), :] = own
        sb[at(base_a, half_rows), :] = own.astype(BF16)
        return [
            send(sb.at[at(base_a + q * block_rows, block_rows)], in_b.at[t, j], peer)
            for j, (q, peer) in enumerate(peers_b)
        ]

    def b_to_c(t, copies):
        _, base_b, _ = starts(t)
        own = add(copies, base_b, block_rows, lambda j: in_b[t, j])
        sums[at(base_b, block_rows), :] = own
        sb[at(base_b, block_rows), :] = own.astype(BF16)
        return [
            send(sb.at[at(base_b + z * chunk, chunk)], in_c.at[t, j], peer)
            for j, (z, peer) in enumerate(peers_c)
        ]

    def c_to_c(t, copies):
        base_c = starts(t)[2]
        full[at(base_c, chunk), :] = add(
            copies, base_c, chunk, lambda j: in_c[t, j]
        ).astype(BF16)
        region = full.at[at(base_c, chunk)]
        return [send(region, region, peer) for _, peer in peers_c]

    def c_to_b(t, copies):
        for copy in copies:
            copy.wait()
        region = full.at[at(starts(t)[1], block_rows)]
        return [send(region, region, peer) for _, peer in peers_b], send(region, region, peer_a)

    def b_to_a(t, copies):
        copies, first = copies
        onward = [first]
        for j, copy in enumerate(copies):
            copy.wait()
            came = lax.rem(quad + groups - 1 - j, groups)
            region = full.at[at(starts(t)[0] + came * block_rows, block_rows)]
            onward.append(send(region, region, peer_a))
        return onward

    turned_back[...] = agm[pl.ds(2, rows)].reshape(rows * width, feats).T
    patch_sums(0, (t0, t1, t2), FINE_UP, rows, turned_back[...])
    fine = start_a(0)

    by_rows(POOL_UP - 1, prows + POOL_UP + 1, pool_one)
    fine = a_to_b(0, fine)
    by_rows(POOL_UP, prows + POOL_UP, pool_two)
    pcol = lax.broadcasted_iota(jnp.int32, (pwidth, feats), 0)
    own_pcols = (pcol >= RIM) & (pcol < pcols + RIM)

    def mask_cot(r, _):
        cm[r] = jnp.where(own_pcols, c0[POOL_UP + r].astype(F32), 0.0).astype(BF16)
        return 0

    lax.fori_loop(0, prows, mask_cot, 0)

    patch_sums(1, (q0, q1, q2), POOL_UP, prows, cm[...].reshape(prows * pwidth, feats).T)
    pool = start_a(1)

    top, one, zero = v0, v1, slope

    def project_fine(i, _):
        y = dot(ag[pl.ds(4 * i, 4)].reshape(4 * width, feats), w1t[...])
        wide = (4, width, feats)
        top[pl.ds(4 * i, 4)] = y[:, 2 * feats :].astype(BF16).astype(F32).reshape(wide)
        one[pl.ds(4 * i, 4)] = y[:, feats : 2 * feats].reshape(wide)
        zero[pl.ds(4 * i, 4)] = y[:, :feats].reshape(wide)
        return 0

    def fine_middle(a):
        def emit(col, half, value):
            at = (a, pl.ds(col, 16), pl.ds(half * LANES, LANES))
            mid[at] = (one[at] + 2.0 * value).astype(BF16).astype(F32)

        stencil(top, coefs, a, a + 4, emit)

    def fine_grad(a):
        def emit(col, half, value):
            at = (a, pl.ds(col, 16), pl.ds(half * LANES, LANES))
            if col + 16 <= RIM + cols:
                out = (a - 2, pl.ds(col - RIM, 16), at[2])
                gp[out] = (zero[at] - top[at] + value).astype(BF16)

        stencil(mid, coefs, a, a + 4, emit, lead=1)

    lax.fori_loop(0, (rows + 4) // 4, project_fine, 0)
    pool = a_to_b(1, pool)
    fine = b_to_c(0, fine)
    by_rows(1, rows + 3, fine_middle)
    fine = c_to_c(0, fine)
    pool = b_to_c(1, pool)
    by_rows(2, rows // 2 + 2, fine_grad)
    fine = c_to_b(0, fine)
    pool = c_to_c(1, pool)
    by_rows(rows // 2 + 2, rows + 2, fine_grad)
    pool = c_to_b(1, pool)

    flat = (prows * pwidth, feats)
    out = dot(q0[pl.ds(POOL_UP, prows)].reshape(flat), w2[0])
    out = out + dot(q1[pl.ds(POOL_UP, prows)].reshape(flat), w2[1])
    out = out + dot(q2[pl.ds(POOL_UP, prows)].reshape(flat), w2[2])
    for r in range(prows):
        start = r * pwidth + RIM
        level[r] = out[start : start + pcols].astype(BF16)

    fine = b_to_a(0, fine)
    pool = b_to_a(1, pool)
    for copy in fine + pool:
        copy.wait()
    for dr, dc, exists, peer in around:
        @pl.when(exists)
        def _():
            for copy in halo_copies(dr, dc, peer)[0]:
                copy().wait_send()


def finish(
    full_in, gp, level, gp_out, gfirst, gsecond, level_out, full, gp_held, level_held, sems
):
    load = pltpu.make_async_copy(full_in, full, sems.at[0])
    load_pixels = pltpu.make_async_copy(gp, gp_held, sems.at[1])
    load_level = pltpu.make_async_copy(level, level_held, sems.at[2])
    pass_pixels = pltpu.make_async_copy(gp_held, gp_out, sems.at[3])
    pass_level = pltpu.make_async_copy(level_held, level_out, sems.at[4])
    for copy in (load, load_pixels, load_level):
        copy.start()
    load_pixels.wait()
    pass_pixels.start()
    load_level.wait()
    pass_level.start()
    load.wait()
    feats = gfirst.shape[1]
    halves = feats // LANES
    batch = full.shape[0] // 2
    count = gfirst.shape[0]
    squares = jnp.zeros((8, LANES), F32)
    for t in range(2):
        x = full[pl.ds(t * batch, count * halves), :].astype(F32)
        squares = squares + jnp.sum((x * x).reshape(count * halves // 8, 8, LANES), axis=0)
    square_sum = jnp.sum(jnp.sum(squares, axis=0, keepdims=True), axis=1, keepdims=True)
    factor = jnp.minimum(1.0, 2.0 * feats * lax.rsqrt(square_sum + 1e-06))
    for t, out in enumerate((gfirst, gsecond)):
        for half in range(halves):
            for k in range(count // feats):
                x = full[pl.ds(t * batch + half * count + k * feats, feats), :].astype(F32)
                out[pl.ds(k * feats + half * LANES, LANES), :] = x.T * factor
    pass_pixels.wait()
    pass_level.wait()


def shards(groups, members, pixels, offsets, first_weights, second_weights, cotangent):
    rows, cols, feats = pixels.shape
    prows, pcols = cotangent.shape[:2]
    width, pwidth = cols + 2 * RIM, pcols + 2 * RIM
    high, phigh, bhigh = rows + 2 * FINE_UP, prows + 2 * POOL_UP, rows + 4
    count = groups * members
    chunk = -(-3 * feats * (feats // LANES) // (count * 16)) * 16
    total = chunk * count
    half = total // 2
    lines = members // 2
    orders = len(STEPS)

    def blocks(n):
        return -(-orders * n // LANES)

    nf, np_ = blocks(rows + 16), blocks(phigh)
    vm = pltpu.VMEM

    def halo(n, up, c):
        return [
            vm((2, n // 2, 16, feats), BF16),
            vm((2, up, c, feats), BF16),
            vm((2, n // 2, 16, feats), BF16),
            vm((4, up // 2, 16, feats), BF16),
        ]

    scratch = [vm((rows, LANES), F32), vm((orders, rows, LANES), F32)]
    scratch += halo(rows, FINE_UP, cols) + halo(prows, POOL_UP, pcols)
    scratch += [
        vm((rows + 16, LANES), F32),
        vm((nf * LANES, LANES), F32), vm((nf, LANES, LANES), F32),
        vm((np_ * LANES, LANES), F32), vm((np_, LANES, LANES), F32),
        vm((orders, high, width, LANES), F32), vm((orders, phigh, pwidth, LANES), F32),
    ]
    scratch += [vm((high, width, feats), t) for t in (BF16, BF16, BF16, F32, F32)]
    scratch += [vm((rows + 8, width, feats), F32)]
    scratch += [vm((phigh, pwidth, feats), BF16), vm((prows, pwidth, feats), BF16)]
    scratch += [vm((phigh, pwidth, feats), t) for t in (BF16,) * 3 + (F32,) * 7]
    scratch += [vm((bhigh, width, feats), t) for t in (BF16, BF16, F32)]
    scratch += [vm((feats, 3 * feats), BF16)] * 2 + [vm((feats, rows * width), BF16)]
    scratch += [
        vm((2 * total, LANES), F32), vm((2 * total, LANES), BF16),
        vm((2, half, LANES), BF16),
        vm((2, groups - 1, half // groups, LANES), BF16),
        vm((2, lines - 1, chunk, LANES), BF16),
    ]
    scratch += [pltpu.SemaphoreType.DMA((3, orders))] * 2
    copies = 2 * (3 * groups + 2 * lines - 3)
    scratch += [pltpu.SemaphoreType.DMA((copies,))] * 2
    held, anywhere = pl.BlockSpec(memory_space=pltpu.VMEM), pl.BlockSpec(memory_space=pl.ANY)
    inner_pixels, full, inner_level = pl.pallas_call(
        functools.partial(kernel, groups, members, chunk),
        out_shape=(
            jax.ShapeDtypeStruct(pixels.shape, BF16),
            jax.ShapeDtypeStruct((2 * total, LANES), BF16),
            jax.ShapeDtypeStruct(cotangent.shape, BF16),
        ),
        in_specs=[held] * 5,
        out_specs=[held] * 3,
        scratch_shapes=scratch,
        compiler_params=pltpu.CompilerParams(
            collective_id=0, has_side_effects=True, vmem_limit_bytes=60 * 1024 * 1024
        ),
    )(pixels, offsets, first_weights, second_weights, cotangent)
    grad_pixels, first, second, level = pl.pallas_call(
        finish,
        out_shape=(
            jax.ShapeDtypeStruct(pixels.shape, BF16),
            jax.ShapeDtypeStruct((3 * feats, feats), F32),
            jax.ShapeDtypeStruct((3 * feats, feats), F32),
            jax.ShapeDtypeStruct(cotangent.shape, BF16),
        ),
        in_specs=[anywhere] * 3,
        out_specs=[anywhere, held, held, anywhere],
        scratch_shapes=[
            vm((2 * total, LANES), BF16), vm(pixels.shape, BF16), vm(cotangent.shape, BF16),
            pltpu.SemaphoreType.DMA((5,)),
        ],
        compiler_params=pltpu.CompilerParams(vmem_limit_bytes=60 * 1024 * 1024),
    )(full, inner_pixels, inner_level)
    shape = first_weights.shape
    return grad_pixels, first.reshape(shape), second.reshape(shape), level


def solution(mesh):
    groups, members = mesh.shape["grp"], mesh.shape["dev"]
    return jax.shard_map(
        functools.partial(shards, groups, members),
        mesh=mesh,
        in_specs=(P("grp", "dev", None), P("grp", "dev"), P(), P(), P("grp", "dev", None)),
        out_specs=(P("grp", "dev", None), P(), P(), P("grp", "dev", None)),
        check_vma=False,
    )
```

```python
import functools

import jax
import jax.numpy as jnp
from jax import lax
from jax.experimental import pallas as pl
from jax.experimental.pallas import tpu as pltpu
from jax.sharding import PartitionSpec as P

MESH = pl.DeviceIdType.MESH
F32 = jnp.float32
BF16 = jnp.bfloat16
STEPS = (
    (-1, 0, 1.0),
    (1, 0, 1.0),
    (0, -1, 1.0),
    (0, 1, 1.0),
    (-1, -1, 0.5),
    (-1, 1, 0.5),
    (1, -1, 0.5),
    (1, 1, 0.5),
)
INDEX = {(dr, dc): k for k, (dr, dc, _) in enumerate(STEPS)}
LANES = 128
RIM = 8
FINE_UP = 6
POOL_UP = 4


def edge_coefficients(offsets, inside):
    rows = offsets.shape[0]

    def moved(x, dr, dc):
        if dr:
            x = pltpu.roll(x, (-dr) % rows, 0)
        if dc:
            x = pltpu.roll(x, (-dc) % LANES, 1)
        return x

    weights = []
    degree = jnp.zeros_like(offsets)
    for dr, dc, coupling in STEPS:
        gap = offsets - moved(offsets, dr, dc)
        weight = coupling * inside * moved(inside, dr, dc) * jnp.exp(-gap * gap)
        weights.append(weight)
        degree = degree + weight
    root = lax.rsqrt(jnp.maximum(degree, 1e-30)) * inside
    found = []
    for (dr, dc, _), weight in zip(STEPS, weights):
        value = -root * weight * moved(root, dr, dc)
        if dc:
            value = pltpu.roll(value, dc % LANES, 1)
        found.append(value)
    return found


def spread_coefficients(found, stack, turned, coefs, shift, first, last):
    rows = found[0].shape[0]
    for k, value in enumerate(found):
        stack[pl.ds(k * rows, rows), :] = value
    for b in range(stack.shape[0] // LANES):
        turned[b] = stack[pl.ds(b * LANES, LANES), :].T
    width = coefs.shape[2]
    for k, step in enumerate(STEPS):
        if step[:2] == (1, 0):
            continue
        for e in range(first, last):
            block, lane = divmod(k * rows + e + shift, LANES)
            coefs[k, e] = jnp.broadcast_to(
                turned[block, pl.ds(0, width), pl.ds(lane, 1)], (width, LANES)
            )


def stencil(values, coefs, row, coef_row, emit, lead=0):
    tiles = values.shape[1] // 8
    halves = values.shape[2] // LANES
    line = lax.broadcasted_iota(jnp.int32, (8, LANES), 0)
    first, last = line == 0, line == 7
    before = [None] * halves
    done = [[] for _ in range(halves)]

    def close(half, left, centre, right, after):
        done[half].append(left + centre + jnp.where(last, after, right))
        j = len(done[half]) - 1
        if j > lead and (j - lead) % 2:
            emit(8 * (j - 1), half, jnp.concatenate(done[half][-2:], axis=0))

    for j in range(tiles):
        cols = pl.ds(8 * j, 8)
        weight = {
            (dr, dc): coefs[k, coef_row, cols]
            for (dr, dc), k in INDEX.items()
            if (dr, dc) != (1, 0)
        }
        weight[1, 0] = coefs[INDEX[-1, 0], coef_row + 1, cols]
        for half in range(halves):
            up, centre, down = (
                values[row + dr, cols, pl.ds(half * LANES, LANES)] for dr in (-1, 0, 1)
            )
            to_right = weight[-1, -1] * up + weight[0, -1] * centre + weight[1, -1] * down
            to_left = weight[-1, 1] * up + weight[0, 1] * centre + weight[1, 1] * down
            straight = weight[-1, 0] * up + weight[1, 0] * down
            to_right = pltpu.roll(to_right, 1, 0)
            to_left = pltpu.roll(to_left, 7, 0)
            left = to_right
            if j:
                old_right, old_left, old_straight, old_to_left = before[half]
                left = jnp.where(first, old_right, to_right)
                close(half, old_left, old_straight, old_to_left, to_left)
            before[half] = (to_right, left, straight, to_left)
    for half in range(halves):
        _, left, straight, to_left = before[half]
        close(half, left, straight, to_left, to_left)


def by_rows(first, last, work):
    def two(i, _):
        work(first + 2 * i)
        work(first + 2 * i + 1)
        return 0

    lax.fori_loop(0, (last - first) // 2, two, 0)
    if (last - first) % 2:
        work(last - 1)


def dot(a, b):
    return lax.dot_general(a, b, (((1,), (0,)), ((), ())), preferred_element_type=F32)


def split_dot(matrix, values):
    value = jnp.concatenate(values, axis=1)
    high = value.astype(BF16)
    low = (value - high.astype(F32)).astype(BF16)
    return dot(matrix, jnp.concatenate([high, low], axis=0))


def kernel(
    groups, members, chunk,
    px, off, w1_in, w2_in, cot,
    gp, full, level,
    off_own, off_in,
    px_pack, px_v, px_h, px_c,
    ct_pack, ct_v, ct_h, ct_c,
    off_ext, stack, turned, pstack, pturned, coefs, pcoefs,
    t0, t1, t2, v0, v1, slope,
    c0, cm, q0, q1, q2, z0, z1, ptop, pone, pzero, pmid, pgrad,
    ag, agm, mid, w1t, w2t, turned_back, w1, w2, weight_sems,
    sums, sb, in_a, in_b, in_c,
    halo_send, halo_recv, sum_send, sum_recv,
):
    rows, cols, feats = px.shape
    prows, pcols = cot.shape[:2]
    width, pwidth = cols + 2 * RIM, pcols + 2 * RIM
    halves = feats // LANES
    g, d = lax.axis_index("grp"), lax.axis_index("dev")

    around = []
    for dr, dc, _ in STEPS:
        ng, nd = g + dr, d + dc
        exists = (ng >= 0) & (ng < groups) & (nd >= 0) & (nd < members)
        around.append((dr, dc, exists, (ng, nd)))
    core, quad, line = lax.rem(g, 2), (g // 2) * 2 + lax.rem(d, 2), d // 2
    lines = members // 2
    peer_a = (g + 1 - 2 * core, d)
    peers_b, peers_c = [], []
    for j in range(1, groups):
        q = lax.rem(quad + j, groups)
        peers_b.append((q, ((q // 2) * 2 + core, line * 2 + lax.rem(q, 2))))
    for j in range(1, lines):
        z = lax.rem(line + j, lines)
        peers_c.append((z, (g, z * 2 + lax.rem(d, 2))))

    fetches = [
        pltpu.make_async_copy(w2_in, w2, weight_sems.at[0]),
        pltpu.make_async_copy(w1_in, w1, weight_sems.at[1]),
    ]
    for copy in fetches:
        copy.start()

    barrier = pltpu.get_barrier_semaphore()
    for dr, dc, exists, peer in around:
        @pl.when(exists)
        def _():
            pl.semaphore_signal(barrier, inc=1, device_id=peer, device_id_type=MESH)
    for peer in [peer_a] + [p for _, p in peers_b] + [p for _, p in peers_c]:
        pl.semaphore_signal(barrier, inc=1, device_id=peer, device_id_type=MESH)

    off_own[...] = jnp.zeros_like(off_own)
    off_own[:, pl.ds(0, cols)] = off[...]
    for source, pack in ((px, px_pack), (cot, ct_pack)):
        edge = source.shape[1]

        def pack_pair(i, _):
            for side, start in ((0, 0), (1, edge - 16)):
                cut = 0 if side == 0 else 8
                parts = [
                    source[2 * i + s, pl.ds(start, 16), :].astype(F32)[cut : cut + 8]
                    for s in (0, 1)
                ]
                pack[side, i] = jnp.concatenate(parts, axis=0).astype(BF16)
            return 0

        lax.fori_loop(0, source.shape[0] // 2, pack_pair, 0)

    greeted = groups + lines - 1
    for dr, dc, exists, peer in around:
        greeted = greeted + jnp.where(exists, 1, 0)
    pl.semaphore_wait(barrier, greeted)

    def halo_copies(dr, dc, peer):
        k, o = INDEX[dr, dc], INDEX[-dr, -dc]
        made = []
        for a, (src, pack, up, v, h, c) in enumerate(
            ((px, px_pack, FINE_UP, px_v, px_h, px_c), (cot, ct_pack, POOL_UP, ct_v, ct_h, ct_c))
        ):
            n = src.shape[0]
            if dc == 0:
                source = src.at[pl.ds(0 if dr < 0 else n - up, up)]
                land, here = v.at[o], v.at[k]
            elif dr == 0:
                source = pack.at[0 if dc < 0 else 1]
                land, here = h.at[o - 2], h.at[k - 2]
            else:
                tiles = up // 2
                source = pack.at[
                    0 if dc < 0 else 1, pl.ds(0 if dr < 0 else n // 2 - tiles, tiles)
                ]
                land, here = c.at[o - 4], c.at[k - 4]
            made.append((a, source, land, here))
        made.append((2, off_own, off_in.at[o], off_in.at[k]))
        outgoing, incoming = [], []
        for a, source, land, here in made:
            copy = functools.partial(
                pltpu.make_async_remote_copy, src_ref=source, send_sem=halo_send.at[a, k],
                device_id=peer, device_id_type=MESH,
            )
            outgoing.append(
                functools.partial(copy, dst_ref=land, recv_sem=halo_recv.at[a, o])
            )
            incoming.append(
                (here, functools.partial(copy, dst_ref=here, recv_sem=halo_recv.at[a, k]))
            )
        return outgoing, incoming

    for a in (2, 1, 0):
        for dr, dc, exists, peer in around:
            @pl.when(exists)
            def _():
                halo_copies(dr, dc, peer)[0][a]().start()

    for dr, dc, exists, peer in around:
        @pl.when(jnp.logical_not(exists))
        def _():
            for here, _ in halo_copies(dr, dc, peer)[1]:
                here[...] = jnp.zeros(here.shape, here.dtype)

    def receive(a):
        for dr, dc, exists, peer in around:
            @pl.when(exists)
            def _():
                halo_copies(dr, dc, peer)[1][a][1]().wait_recv()

    for copy, source, target in zip(fetches, (w2, w1), (w2t, w1t)):
        copy.wait()
        for k in range(source.shape[0]):
            target[:, pl.ds(k * feats, feats)] = source[k].T
    receive(2)

    def lay(left, own, right):
        lane = lax.broadcasted_iota(jnp.int32, own.shape, 1)
        out = jnp.where(lane < RIM, pltpu.roll(left, (RIM - cols) % LANES, 1), 0.0)
        out = jnp.where((lane >= RIM) & (lane < cols + RIM), pltpu.roll(own, RIM, 1), out)
        return jnp.where(
            (lane >= cols + RIM) & (lane < width), pltpu.roll(right, cols + RIM, 1), out
        )

    def slot(dr, dc, cut):
        return off_in[INDEX[dr, dc], cut, :]

    high, low = pl.ds(rows - 8, 8), pl.ds(0, 8)
    off_ext[pl.ds(0, 8), :] = lay(slot(-1, -1, high), slot(-1, 0, high), slot(-1, 1, high))
    off_ext[pl.ds(8, rows), :] = lay(off_in[INDEX[0, -1]], off_own[...], off_in[INDEX[0, 1]])
    off_ext[pl.ds(8 + rows, 8), :] = lay(slot(1, -1, low), slot(1, 0, low), slot(1, 1, low))

    def within(shape, row_start, col_start, row_end, col_end, used):
        r = lax.broadcasted_iota(jnp.int32, shape, 0) + row_start
        lane = lax.broadcasted_iota(jnp.int32, shape, 1)
        c = lane + col_start
        ok = (r >= 0) & (r < row_end) & (c >= 0) & (c < col_end) & (lane < used)
        return jnp.where(ok, 1.0, 0.0).astype(F32)

    offsets = off_ext[...]
    inside = within(
        offsets.shape, g * rows - 8, d * cols - RIM, groups * rows, members * cols, width
    )
    pshape = (prows + 2 * POOL_UP, LANES)
    a_r = lax.broadcasted_iota(jnp.int32, (pshape[0], rows + 16), 0)
    a_f = lax.broadcasted_iota(jnp.int32, (pshape[0], rows + 16), 1)
    by_row = jnp.where((a_f == 2 * a_r) | (a_f == 2 * a_r + 1), 0.5, 0.0).astype(F32)
    b_f = lax.broadcasted_iota(jnp.int32, (LANES, LANES), 0)
    b_l = lax.broadcasted_iota(jnp.int32, (LANES, LANES), 1)
    by_col = jnp.where((b_f == 2 * b_l - 8) | (b_f == 2 * b_l - 7), 0.5, 0.0).astype(F32)
    exact = functools.partial(
        jnp.dot, precision=lax.Precision.HIGHEST, preferred_element_type=F32
    )
    poffsets = exact(exact(by_row, offsets), by_col)
    pinside = within(
        pshape, g * prows - POOL_UP, d * pcols - RIM, groups * prows, members * pcols, pwidth
    )
    spread_coefficients(
        edge_coefficients(poffsets, pinside), pstack, pturned, pcoefs, 0, 1,
        prows + 2 * POOL_UP,
    )

    def assemble(store, start, pairs, middle, left, right):
        def pair(i, _):
            lt, rt = left(i).astype(F32), right(i).astype(F32)
            for s in (0, 1):
                row = jnp.concatenate(
                    [
                        lt[8 * s : 8 * s + 8],
                        middle(2 * i + s).astype(F32),
                        rt[8 * s : 8 * s + 8],
                    ],
                    axis=0,
                )
                store(start + 2 * i + s, row)
            return 0

        lax.fori_loop(0, pairs, pair, 0)

    def store_px(e, row):
        v0[e] = row
        t0[e] = row.astype(BF16)

    def store_cot(e, row):
        c0[e] = row.astype(BF16)

    def assemble_all(store, src, up, v, h, c):
        n = src.shape[0]
        assemble(store, 0, up // 2, lambda r: v[0, r], lambda i: c[0, i], lambda i: c[1, i])
        assemble(store, up, n // 2, lambda r: src[r], lambda i: h[0, i], lambda i: h[1, i])
        assemble(store, up + n, up // 2, lambda r: v[1, r], lambda i: c[2, i], lambda i: c[3, i])

    receive(1)
    assemble_all(store_cot, cot, POOL_UP, ct_v, ct_h, ct_c)

    def project_pool(i, _):
        y = dot(c0[pl.ds(4 * i, 4)].reshape(4 * pwidth, feats), w2t[...])
        wide = (4, pwidth, feats)
        ptop[pl.ds(4 * i, 4)] = y[:, 2 * feats :].astype(BF16).astype(F32).reshape(wide)
        pone[pl.ds(4 * i, 4)] = y[:, feats : 2 * feats].reshape(wide)
        pzero[pl.ds(4 * i, 4)] = y[:, :feats].reshape(wide)
        return 0

    lax.fori_loop(0, (prows + 2 * POOL_UP) // 4, project_pool, 0)

    def pool_middle(e):
        def emit(col, half, value):
            at = (e, pl.ds(col, 16), pl.ds(half * LANES, LANES))
            pmid[at] = (pone[at] + 2.0 * value).astype(BF16).astype(F32)

        stencil(ptop, pcoefs, e, e, emit)

    def pool_grad(e):
        def emit(col, half, value):
            at = (e, pl.ds(col, 16), pl.ds(half * LANES, LANES))
            pgrad[at] = pzero[at] - ptop[at] + value

        stencil(pmid, pcoefs, e, e, emit)

    by_rows(2, prows + 2 * POOL_UP - 2, pool_middle)
    by_rows(3, prows + 2 * POOL_UP - 3, pool_grad)

    spread_coefficients(
        edge_coefficients(offsets, inside), stack, turned, coefs, 2, 1, rows + 2 * FINE_UP
    )
    receive(0)
    assemble_all(store_px, px, FINE_UP, px_v, px_h, px_c)

    def fine_one(e):
        def emit(col, half, value):
            at = (e, pl.ds(col, 16), pl.ds(half * LANES, LANES))
            value = value.astype(BF16)
            t1[at] = value
            v1[at] = value.astype(F32)

        stencil(v0, coefs, e, e, emit)

    def fine_two(e):
        def emit(col, half, value):
            at = (e, pl.ds(col, 16), pl.ds(half * LANES, LANES))
            t2[at] = (2.0 * value - v0[at]).astype(BF16)

        stencil(v1, coefs, e, e, emit)

    by_rows(1, rows + 2 * FINE_UP - 1, fine_one)
    by_rows(2, rows + 2 * FINE_UP - 2, fine_two)

    def pool_matrix(shape, fine_dim, repeat):
        f = lax.broadcasted_iota(jnp.int32, shape, fine_dim)
        p = lax.broadcasted_iota(jnp.int32, shape, 1 - fine_dim)
        f, p = (lax.rem(f, repeat), p) if fine_dim else (f, lax.rem(p, repeat))
        return jnp.where((f == 2 * p - 8) | (f == 2 * p - 7), 0.25, 0.0).astype(BF16)

    gather_pool = pool_matrix((pwidth, 2 * width), 1, width)
    spread_pool = pool_matrix((width, 2 * pwidth), 0, pwidth)

    def activate(i, _):
        e = 2 + 4 * i
        flat = (4 * width, feats)
        a = dot(t0[pl.ds(e, 4)].reshape(flat), w1[0])
        a = a + dot(t1[pl.ds(e, 4)].reshape(flat), w1[1])
        a = a + dot(t2[pl.ds(e, 4)].reshape(flat), w1[2])
        s = jax.nn.sigmoid(a)
        slope[pl.ds(4 * i, 4)] = (s * (1.0 + a * (1.0 - s))).reshape(4, width, feats)
        hidden = a * s
        both = [
            hidden[2 * p * width : (2 * p + 1) * width]
            + hidden[(2 * p + 1) * width : (2 * p + 2) * width]
            for p in (0, 1)
        ]
        value = split_dot(gather_pool, both).astype(BF16)
        for p in (0, 1):
            part = value[:, p * feats : (p + 1) * feats]
            q0[2 + 2 * i + p] = part
            z0[2 + 2 * i + p] = part.astype(F32)
        return 0

    lax.fori_loop(0, (prows + 4) // 2, activate, 0)

    col = lax.broadcasted_iota(jnp.int32, (width, feats), 0)
    own_cols = (col >= RIM) & (col < cols + RIM)

    def act_grad(i, _):
        wide = split_dot(spread_pool, [pgrad[3 + 2 * i], pgrad[4 + 2 * i]])
        for r in range(4):
            value = wide[:, (r // 2) * feats : (r // 2 + 1) * feats] * slope[4 * i + 2 + r]
            ag[4 * i + r] = value.astype(BF16)
            agm[4 * i + r] = jnp.where(own_cols, value, 0.0).astype(BF16)
        return 0

    lax.fori_loop(0, (prows + 2) // 2, act_grad, 0)

    def pool_one(e):
        def emit(col, half, value):
            at = (e, pl.ds(col, 16), pl.ds(half * LANES, LANES))
            value = value.astype(BF16)
            q1[at] = value
            z1[at] = value.astype(F32)

        stencil(z0, pcoefs, e, e, emit)

    def pool_two(e):
        def emit(col, half, value):
            at = (e, pl.ds(col, 16), pl.ds(half * LANES, LANES))
            q2[at] = (2.0 * value - z0[at]).astype(BF16)

        stencil(z1, pcoefs, e, e, emit)

    batch = sums.shape[0] // 2
    half_rows = batch // 2
    block_rows = half_rows // groups
    parts = 3 * feats * halves

    def at(start, size):
        return pl.ds(pl.multiple_of(start, 16), size)

    numbers = iter(range(sum_send.shape[0]))

    def send(source, target, peer):
        number = next(numbers)
        copy = pltpu.make_async_remote_copy(
            src_ref=source, dst_ref=target, send_sem=sum_send.at[number],
            recv_sem=sum_recv.at[number], device_id=peer, device_id_type=MESH,
        )
        copy.start()
        return copy

    def starts(t):
        base_a = t * batch + core * half_rows
        base_b = base_a + quad * block_rows
        return base_a, base_b, base_b + line * chunk

    def patch_sums(t, terms, first, count, back):
        if batch > parts:
            rest = batch - parts
            sb[pl.ds(t * batch + parts, rest), :] = jnp.zeros((rest, LANES), BF16)
            sums[pl.ds(t * batch + parts, rest), :] = jnp.zeros((rest, LANES), F32)
        for k, term in enumerate(terms):
            x = term[pl.ds(first, count)].reshape(back.shape[1], feats)
            value = dot(back, x)
            for half in range(halves):
                place = pl.ds(t * batch + (half * 3 + k) * feats, feats)
                part = value[:, half * LANES : (half + 1) * LANES]
                sums[place, :] = part
                sb[place, :] = part.astype(BF16)

    def start_a(t):
        other = at(t * batch + (1 - core) * half_rows, half_rows)
        return [send(sb.at[other], in_a.at[t], peer_a)]

    def add(copies, start, size, landed):
        for copy in copies:
            copy.wait()
        own = sums[at(start, size), :]
        for j in range(len(copies)):
            own = own + landed(j).astype(F32)
        return own

    def a_to_b(t, copies):
        base_a, base_b, _ = starts(t)
        own = add(copies, base_a, half_rows, lambda j: in_a[t])
        sums[at(base_a, half_rows), :] = own
        sb[at(base_a, half_rows), :] = own.astype(BF16)
        return [
            send(sb.at[at(base_a + q * block_rows, block_rows)], in_b.at[t, j], peer)
            for j, (q, peer) in enumerate(peers_b)
        ]

    def b_to_c(t, copies):
        _, base_b, _ = starts(t)
        own = add(copies, base_b, block_rows, lambda j: in_b[t, j])
        sums[at(base_b, block_rows), :] = own
        sb[at(base_b, block_rows), :] = own.astype(BF16)
        return [
            send(sb.at[at(base_b + z * chunk, chunk)], in_c.at[t, j], peer)
            for j, (z, peer) in enumerate(peers_c)
        ]

    def c_to_c(t, copies):
        base_c = starts(t)[2]
        full[at(base_c, chunk), :] = add(
            copies, base_c, chunk, lambda j: in_c[t, j]
        ).astype(BF16)
        region = full.at[at(base_c, chunk)]
        return [send(region, region, peer) for _, peer in peers_c]

    def c_to_b(t, copies):
        for copy in copies:
            copy.wait()
        region = full.at[at(starts(t)[1], block_rows)]
        return [send(region, region, peer) for _, peer in peers_b], send(region, region, peer_a)

    def b_to_a(t, copies):
        copies, first = copies
        onward = [first]
        for j, copy in enumerate(copies):
            copy.wait()
            came = lax.rem(quad + groups - 1 - j, groups)
            region = full.at[at(starts(t)[0] + came * block_rows, block_rows)]
            onward.append(send(region, region, peer_a))
        return onward

    turned_back[...] = agm[pl.ds(2, rows)].reshape(rows * width, feats).T
    patch_sums(0, (t0, t1, t2), FINE_UP, rows, turned_back[...])
    fine = start_a(0)

    by_rows(POOL_UP - 1, prows + POOL_UP + 1, pool_one)
    fine = a_to_b(0, fine)
    by_rows(POOL_UP, prows + POOL_UP, pool_two)
    pcol = lax.broadcasted_iota(jnp.int32, (pwidth, feats), 0)
    own_pcols = (pcol >= RIM) & (pcol < pcols + RIM)

    def mask_cot(r, _):
        cm[r] = jnp.where(own_pcols, c0[POOL_UP + r].astype(F32), 0.0).astype(BF16)
        return 0

    lax.fori_loop(0, prows, mask_cot, 0)

    patch_sums(1, (q0, q1, q2), POOL_UP, prows, cm[...].reshape(prows * pwidth, feats).T)
    pool = start_a(1)

    top, one, zero = v0, v1, slope

    def project_fine(i, _):
        y = dot(ag[pl.ds(4 * i, 4)].reshape(4 * width, feats), w1t[...])
        wide = (4, width, feats)
        top[pl.ds(4 * i, 4)] = y[:, 2 * feats :].astype(BF16).astype(F32).reshape(wide)
        one[pl.ds(4 * i, 4)] = y[:, feats : 2 * feats].reshape(wide)
        zero[pl.ds(4 * i, 4)] = y[:, :feats].reshape(wide)
        return 0

    def fine_middle(a):
        def emit(col, half, value):
            at = (a, pl.ds(col, 16), pl.ds(half * LANES, LANES))
            mid[at] = (one[at] + 2.0 * value).astype(BF16).astype(F32)

        stencil(top, coefs, a, a + 4, emit)

    def fine_grad(a):
        def emit(col, half, value):
            at = (a, pl.ds(col, 16), pl.ds(half * LANES, LANES))
            if col + 16 <= RIM + cols:
                out = (a - 2, pl.ds(col - RIM, 16), at[2])
                gp[out] = (zero[at] - top[at] + value).astype(BF16)

        stencil(mid, coefs, a, a + 4, emit, lead=1)

    lax.fori_loop(0, (rows + 4) // 4, project_fine, 0)
    pool = a_to_b(1, pool)
    fine = b_to_c(0, fine)
    by_rows(1, rows + 3, fine_middle)
    fine = c_to_c(0, fine)
    pool = b_to_c(1, pool)
    by_rows(2, rows // 2 + 2, fine_grad)
    fine = c_to_b(0, fine)
    pool = c_to_c(1, pool)
    by_rows(rows // 2 + 2, rows + 2, fine_grad)
    pool = c_to_b(1, pool)

    flat = (prows * pwidth, feats)
    out = dot(q0[pl.ds(POOL_UP, prows)].reshape(flat), w2[0])
    out = out + dot(q1[pl.ds(POOL_UP, prows)].reshape(flat), w2[1])
    out = out + dot(q2[pl.ds(POOL_UP, prows)].reshape(flat), w2[2])
    for r in range(prows):
        start = r * pwidth + RIM
        level[r] = out[start : start + pcols].astype(BF16)

    fine = b_to_a(0, fine)
    pool = b_to_a(1, pool)
    for copy in fine + pool:
        copy.wait()
    for dr, dc, exists, peer in around:
        @pl.when(exists)
        def _():
            for copy in halo_copies(dr, dc, peer)[0]:
                copy().wait_send()


def finish(
    full_in, gp, level, gp_out, gfirst, gsecond, level_out, full, gp_held, level_held,
    scaled, sems, out_sems,
):
    load = pltpu.make_async_copy(full_in, full, sems.at[0])
    load_pixels = pltpu.make_async_copy(gp, gp_held, sems.at[1])
    load_level = pltpu.make_async_copy(level, level_held, sems.at[2])
    pass_pixels = pltpu.make_async_copy(gp_held, gp_out, sems.at[3])
    pass_level = pltpu.make_async_copy(level_held, level_out, sems.at[4])
    for copy in (load, load_pixels, load_level):
        copy.start()
    load_pixels.wait()
    pass_pixels.start()
    load_level.wait()
    pass_level.start()
    load.wait()
    feats = gfirst.shape[1]
    halves = feats // LANES
    batch = full.shape[0] // 2
    count = gfirst.shape[0]
    squares = jnp.zeros((8, LANES), F32)
    for t in range(2):
        x = full[pl.ds(t * batch, count * halves), :].astype(F32)
        squares = squares + jnp.sum((x * x).reshape(count * halves // 8, 8, LANES), axis=0)
    square_sum = jnp.sum(jnp.sum(squares, axis=0, keepdims=True), axis=1, keepdims=True)
    factor = jnp.minimum(1.0, 2.0 * feats * lax.rsqrt(square_sum + 1e-06))
    sent = []
    for t, out in enumerate((gfirst, gsecond)):
        for k in range(count // feats):
            place = pl.ds(k * feats, feats)
            for half in range(halves):
                x = full[pl.ds(t * batch + half * count + k * feats, feats), :].astype(F32)
                scaled[t, pl.ds(k * feats + half * LANES, LANES), :] = x.T * factor
            sent.append(
                pltpu.make_async_copy(scaled.at[t, place], out.at[place], out_sems.at[t, k])
            )
            sent[-1].start()
    for copy in sent:
        copy.wait()
    pass_pixels.wait()
    pass_level.wait()


def shards(groups, members, pixels, offsets, first_weights, second_weights, cotangent):
    rows, cols, feats = pixels.shape
    prows, pcols = cotangent.shape[:2]
    width, pwidth = cols + 2 * RIM, pcols + 2 * RIM
    high, phigh, bhigh = rows + 2 * FINE_UP, prows + 2 * POOL_UP, rows + 4
    count = groups * members
    chunk = -(-3 * feats * (feats // LANES) // (count * 16)) * 16
    total = chunk * count
    half = total // 2
    lines = members // 2
    orders = len(STEPS)

    def blocks(n):
        return -(-orders * n // LANES)

    nf, np_ = blocks(rows + 16), blocks(phigh)
    vm = pltpu.VMEM

    def halo(n, up, c):
        return [
            vm((2, n // 2, 16, feats), BF16),
            vm((2, up, c, feats), BF16),
            vm((2, n // 2, 16, feats), BF16),
            vm((4, up // 2, 16, feats), BF16),
        ]

    scratch = [vm((rows, LANES), F32), vm((orders, rows, LANES), F32)]
    scratch += halo(rows, FINE_UP, cols) + halo(prows, POOL_UP, pcols)
    scratch += [
        vm((rows + 16, LANES), F32),
        vm((nf * LANES, LANES), F32), vm((nf, LANES, LANES), F32),
        vm((np_ * LANES, LANES), F32), vm((np_, LANES, LANES), F32),
        vm((orders, high, width, LANES), F32), vm((orders, phigh, pwidth, LANES), F32),
    ]
    scratch += [vm((high, width, feats), t) for t in (BF16, BF16, BF16, F32, F32)]
    scratch += [vm((rows + 8, width, feats), F32)]
    scratch += [vm((phigh, pwidth, feats), BF16), vm((prows, pwidth, feats), BF16)]
    scratch += [vm((phigh, pwidth, feats), t) for t in (BF16,) * 3 + (F32,) * 7]
    scratch += [vm((bhigh, width, feats), t) for t in (BF16, BF16, F32)]
    scratch += [vm((feats, 3 * feats), BF16)] * 2 + [vm((feats, rows * width), BF16)]
    scratch += [vm(first_weights.shape, BF16)] * 2 + [pltpu.SemaphoreType.DMA((2,))]
    scratch += [
        vm((2 * total, LANES), F32), vm((2 * total, LANES), BF16),
        vm((2, half, LANES), BF16),
        vm((2, groups - 1, half // groups, LANES), BF16),
        vm((2, lines - 1, chunk, LANES), BF16),
    ]
    scratch += [pltpu.SemaphoreType.DMA((3, orders))] * 2
    copies = 2 * (3 * groups + 2 * lines - 3)
    scratch += [pltpu.SemaphoreType.DMA((copies,))] * 2
    held, anywhere = pl.BlockSpec(memory_space=pltpu.VMEM), pl.BlockSpec(memory_space=pl.ANY)
    inner_pixels, full, inner_level = pl.pallas_call(
        functools.partial(kernel, groups, members, chunk),
        out_shape=(
            jax.ShapeDtypeStruct(pixels.shape, BF16),
            jax.ShapeDtypeStruct((2 * total, LANES), BF16),
            jax.ShapeDtypeStruct(cotangent.shape, BF16),
        ),
        in_specs=[held, held, anywhere, anywhere, held],
        out_specs=[held] * 3,
        scratch_shapes=scratch,
        compiler_params=pltpu.CompilerParams(
            collective_id=0, has_side_effects=True, vmem_limit_bytes=60 * 1024 * 1024
        ),
    )(pixels, offsets, first_weights, second_weights, cotangent)
    grad_pixels, first, second, level = pl.pallas_call(
        finish,
        out_shape=(
            jax.ShapeDtypeStruct(pixels.shape, BF16),
            jax.ShapeDtypeStruct((3 * feats, feats), F32),
            jax.ShapeDtypeStruct((3 * feats, feats), F32),
            jax.ShapeDtypeStruct(cotangent.shape, BF16),
        ),
        in_specs=[anywhere] * 3,
        out_specs=[anywhere] * 4,
        scratch_shapes=[
            vm((2 * total, LANES), BF16), vm(pixels.shape, BF16), vm(cotangent.shape, BF16),
            vm((2, 3 * feats, feats), F32),
            pltpu.SemaphoreType.DMA((5,)), pltpu.SemaphoreType.DMA((2, 3)),
        ],
        compiler_params=pltpu.CompilerParams(vmem_limit_bytes=60 * 1024 * 1024),
    )(full, inner_pixels, inner_level)
    shape = first_weights.shape
    return grad_pixels, first.reshape(shape), second.reshape(shape), level


def solution(mesh):
    groups, members = mesh.shape["grp"], mesh.shape["dev"]
    return jax.shard_map(
        functools.partial(shards, groups, members),
        mesh=mesh,
        in_specs=(P("grp", "dev", None), P("grp", "dev"), P(), P(), P("grp", "dev", None)),
        out_specs=(P("grp", "dev", None), P(), P(), P("grp", "dev", None)),
        check_vma=False,
    )
```
